128 devices in a mesh: row: 8 (over x, z_hi), col: 16 (over z_lo, y, core).
Axes of the slice: x: 4, y: 4, z: 4 (z_hi: 2, z_lo: 2; z = z_hi * 2 + z_lo), core: 2. Of those that a mesh axis runs over, the one named last changes fastest.
Arguments:
- features: bfloat16 [2, 512, 2048, 128], P(None, 'row', 'col'), may hold values from -18 to 18
- grad_out: bfloat16 [2, 512, 2048, 128], P(None, 'row', 'col'), may hold values from -6 to 6
- w_qkv: bfloat16 [128, 384], replicated, may hold values from -3 to 3
- w_out: bfloat16 [128, 128], replicated, may hold values from -0.5 to 0.5
- cross_live: int32 [64, 256], P('row', 'col'), may hold values 0 or 1
- route: int32 [8, 16, 16, 8], P('row', 'col'), may hold values from -1 to 127, as said below
Outputs:
- grad_features: float32 [2, 512, 2048, 128], P(None, 'row', 'col')
The draws below stay inside these ranges and needn't reach their ends.
Inputs may be any that keep to these rules, and one draw needn't show every extreme that they name: Each route[i, j, d, :] is either all -1 or 8 distinct window indices of tile (i, j); no window of a tile is listed twice; every tile (i, d) is named by exactly 8 source tiles of row i, so it computes exactly 64 windows.
All inputs are finite; a program needn't handle non-finite values. No bound on the sum of `cross_live` on one device may be relied on, other than what follows from the above.
Results may differ from the reference program's by a relative error of at most 0.0003.
Values may be sent and summed in bfloat16 or wider, within the bound.
No kernel may reach another device: no remote copies, remote signals or barrier semaphores. Data moves between devices by JAX's collectives and lax.ppermute only.
A program may use at most 128 MiB of HBM per device.

```python
import math
import jax
import jax.numpy as jnp
from jax import lax

C = 128
HEADS = 4
WIN = 8
TH = 64
TW = 128
CAP = 8
PER = 8
LOADS = 64
H = 512
W = 2048
WIN_DEV = 128
N_ROW = 8
N_COL = 16


def draw_features(key, part):
    key = jax.random.fold_in(key, 3)
    key_base = jax.random.fold_in(key, 0)
    base_noise = jnp.clip(jax.random.normal(key_base, (2, H, W, C), jnp.float32), -6.0, 6.0)
    return base_noise.astype(jnp.bfloat16)


def draw_w_qkv(key, part):
    key = jax.random.fold_in(key, 5)
    matrix = jnp.clip(jax.random.normal(key, (C, 3 * C), jnp.float32), -6.0, 6.0) * C ** (-0.5)
    return matrix.astype(jnp.bfloat16)


def draw_route(key, part):
    key = jax.random.fold_in(key, 11)
    key_shift, key_sign, key_perm = jax.random.split(key, 3)
    shifts = jax.random.randint(key_shift, (N_ROW, N_COL // 2), 0, PER)
    signs = jax.random.randint(key_sign, (N_ROW, N_COL // 2), 0, 2) * 2 - 1
    counts = jnp.concatenate([PER + signs * shifts, PER - signs * shifts], axis=1)
    starts = jnp.cumsum(counts, axis=1) - counts
    destination = jnp.arange(N_COL)[None, None, :]
    rank_in = (destination - starts[:, :, None]) % N_COL
    active = rank_in < counts[:, :, None]
    perm_keys = jax.random.split(key_perm, N_ROW * N_COL)
    orders = jax.vmap(lambda sub_key: jax.random.permutation(sub_key, WIN_DEV))(perm_keys)
    orders = orders.reshape(N_ROW, N_COL, 1, WIN_DEV)
    orders = jnp.broadcast_to(orders, (N_ROW, N_COL, N_COL, WIN_DEV))
    slot_pos = rank_in[..., None] * CAP + jnp.arange(CAP)[None, None, None, :]
    slot_pos = jnp.minimum(slot_pos, WIN_DEV - 1)
    picked = jnp.take_along_axis(orders, slot_pos, axis=3)
    return jnp.where(active[..., None], picked, -1).astype(jnp.int32)


def set_ends(result, key, low, top_value):
    dims = result.shape
    spot = [jax.random.randint(jax.random.fold_in(key, axis), (), 0, dims[axis]) for axis in range(len(dims))]
    result = result.at[tuple(spot)].set(low)
    longest = dims.index(max(dims))
    spot[longest] = (spot[longest] + 1) % dims[longest]
    return result.at[tuple(spot)].set(top_value)


def levels(key, extent, pieces, least, top_value):
    factor_of, own = 1.0, jax.random.fold_in(key, 6)
    for axis_at, shards_of in pieces:
        draws = jnp.exp(jax.random.uniform(jax.random.fold_in(own, axis_at), (shards_of,), jnp.float32, least / len(pieces), top_value / len(pieces)))
        factor_of = factor_of * jnp.repeat(draws, extent[axis_at] // shards_of).reshape([-1 if axis == axis_at else 1 for axis in range(len(extent))])
    return factor_of


def gaussian(rng, dims, spread, bound, cuts=(), kind=jnp.bfloat16):
    gain = levels(rng, dims, cuts, -0.22, 0.18) if cuts else 1.0
    values = jax.random.normal(rng, dims, jnp.float32) * spread * gain
    return jnp.minimum(jnp.maximum(values, -bound), bound).astype(kind)


def setup_inputs(seed: int = 0) -> dict:
    key_of = jax.random.split(jax.random.key(seed), 7)
    features = draw_features(jax.random.fold_in(key_of[6], 71), 0)
    grad_out = gaussian(key_of[1], (2, H, W, C), 1.0, 6.0, ((1, 8), (2, 16)))
    w_qkv = draw_w_qkv(jax.random.fold_in(key_of[6], 71), 0)
    w_out = gaussian(key_of[3], (C, C), C ** -0.5, 0.5)
    cross_live = set_ends((jax.random.randint(key_of[4], (H // WIN, W // WIN), 0, 4) < 3).astype(jnp.int32), jax.random.fold_in(key_of[4], 1), 0, 1)
    route = draw_route(jax.random.fold_in(key_of[6], 71), 0)
    return {"features": features, "grad_out": grad_out, "w_qkv": w_qkv, "w_out": w_out, "cross_live": cross_live, "route": route}


def window_out(window_feat, cross_flag, w_in, w_proj):
    window_count, view_count, token_count, feat_width = window_feat.shape
    head_size = feat_width // HEADS
    projected = jnp.einsum('bvtc,cd->bvtd', window_feat, w_in, precision=lax.Precision.HIGHEST)
    queries = projected[..., :feat_width]
    key_rows = projected[..., feat_width:2 * feat_width]
    valued = projected[..., 2 * feat_width:]
    key_rows = jnp.concatenate([key_rows, key_rows[:, ::-1]], axis=2)
    valued = jnp.concatenate([valued, valued[:, ::-1]], axis=2)
    queries = queries.reshape(window_count, view_count, token_count, HEADS, head_size)
    key_rows = key_rows.reshape(window_count, view_count, 2 * token_count, HEADS, head_size)
    valued = valued.reshape(window_count, view_count, 2 * token_count, HEADS, head_size)
    scores = jnp.einsum('bvqhd,bvkhd->bvhqk', queries, key_rows, precision=lax.Precision.HIGHEST) * head_size ** (-0.5)
    own_key = jnp.arange(2 * token_count) < token_count
    keep_key = own_key[None, :] | (cross_flag[:, None] > 0)
    scores = jnp.where(keep_key[:, None, None, None, :], scores, -1e+30)
    row_max = lax.stop_gradient(lax.optimization_barrier(jnp.max(scores, axis=-1, keepdims=True)))
    weights = jnp.exp(scores - row_max)
    weights = weights / lax.optimization_barrier(jnp.sum(weights, axis=-1, keepdims=True))
    attended = jnp.einsum('bvhqk,bvkhd->bvqhd', weights, valued, precision=lax.Precision.HIGHEST)
    attended = attended.reshape(window_count, view_count, token_count, feat_width)
    return jnp.einsum('bvtc,cd->bvtd', attended, w_proj, precision=lax.Precision.HIGHEST)

def window_grads(feat_block, grad_block, flag_block, w_in, w_proj):

    def forward(window_feat):
        return window_out(window_feat, flag_block, w_in, w_proj)
    _, pull_back = jax.vjp(forward, feat_block.astype(jnp.float32))
    return pull_back(grad_block.astype(jnp.float32))[0]

def to_windows(image_tile):
    view_count, row_count, col_count, feat_width = image_tile.shape
    shaped = image_tile.reshape(view_count, row_count // WIN, WIN, col_count // WIN, WIN, feat_width)
    return shaped.transpose(1, 3, 0, 2, 4, 5).reshape(-1, view_count, WIN * WIN, feat_width)

def from_windows(window_blocks, row_count, col_count):
    view_count = window_blocks.shape[1]
    feat_width = window_blocks.shape[3]
    shaped = window_blocks.reshape(row_count // WIN, col_count // WIN, view_count, WIN, WIN, feat_width)
    return shaped.transpose(2, 0, 3, 1, 4, 5).reshape(view_count, row_count, col_count, feat_width)

def reference(features, grad_out, w_qkv, w_out, cross_live, route):
    half_win = WIN // 2
    rolled = jnp.roll(features, (-half_win, -half_win), axis=(1, 2))
    rolled_grad = jnp.roll(grad_out, (-half_win, -half_win), axis=(1, 2))
    windows = to_windows(rolled)
    grad_windows = to_windows(rolled_grad)
    tile_rows = TH // WIN
    tile_cols = TW // WIN
    grid_cols = W // WIN
    row_index = jnp.arange(N_ROW, dtype=jnp.int32)[:, None, None, None]
    col_index = jnp.arange(N_COL, dtype=jnp.int32)[None, :, None, None]
    global_ids = (row_index * tile_rows + route // tile_cols) * grid_cols + col_index * tile_cols + route % tile_cols
    flat_route = route.reshape(-1)
    flat_global = global_ids.reshape(-1)
    total_count = N_ROW * N_COL * LOADS
    chosen = jnp.nonzero(flat_route >= 0, size=total_count)[0]
    live_ids = flat_global[chosen].astype(jnp.int32)
    cross_flat = cross_live.reshape(-1)
    w_in = w_qkv.astype(jnp.float32)
    w_proj = w_out.astype(jnp.float32)
    block_size = math.gcd(total_count, 32)

    def per_block(block_ids):
        return window_grads(windows[block_ids], grad_windows[block_ids], cross_flat[block_ids], w_in, w_proj)
    grads = lax.map(per_block, live_ids.reshape(total_count // block_size, block_size))
    grads = grads.reshape((total_count,) + windows.shape[1:])
    placed = jnp.zeros(windows.shape, jnp.float32).at[live_ids].set(grads)
    image_grad = from_windows(placed, H, W)
    return jnp.roll(image_grad, (half_win, half_win), axis=(1, 2))
```

```python
import functools
import math

import jax
import jax.numpy as jnp
from jax import lax
from jax.experimental import pallas as pl
from jax.experimental.pallas import tpu as pltpu
from jax.sharding import PartitionSpec as P

F32 = jnp.float32
BF16 = jnp.bfloat16
HEADS = 4
WIN = 8
HALF = 4
CH = 128
HEAD = CH // HEADS
TOK = WIN * WIN
GROUP = 4
NEG = -1e30
LOG2E = math.log2(math.e)
SCALE = 1.0 / math.sqrt(HEAD)


def split(value):
    high = value.astype(BF16)
    return high, (value - high.astype(F32)).astype(BF16)


def mm(a, b):
    return lax.dot_general(a, b, (((1,), (0,)), ((), ())), preferred_element_type=F32)


def mm_nt(a, b):
    return lax.dot_general(a, b, (((1,), (1,)), ((), ())), preferred_element_type=F32)


def cat(parts, axis):
    return jnp.concatenate(parts, axis=axis)


def head_pair_rows(high, low, pair):
    zero = jnp.zeros((HEAD, 2 * TOK), BF16)
    zeros = jnp.zeros((2 * HEAD, 4 * TOK), BF16)
    first, second = (slice(HEAD * h, HEAD * h + HEAD) for h in (2 * pair, 2 * pair + 1))
    top = [cat([high[first], zero], 1), cat([zero, high[second]], 1)]
    fix = [cat([low[first], zero], 1), cat([zero, low[second]], 1)]
    tail = fix + [zeros] if pair == 0 else [zeros] + fix
    return cat(top + top + tail, 0)


def pair_product(tokens, columns, pair):
    lanes = slice(2 * HEAD * pair, 2 * HEAD * pair + 2 * HEAD)
    left = cat([tokens[0][:, lanes], tokens[1][:, lanes], tokens[0]], 1)
    return mm(left, head_pair_rows(columns[0], columns[1], pair))


class Window:
    def __init__(self, across, along, flag):
        self.q_t = split(across[:CH] * (LOG2E * SCALE))
        self.k_t = split(across[CH : 2 * CH])
        self.a_t = split(across[2 * CH :])
        self.k, self.v, self.q, self.a = (
            split(along[:, CH * n : CH * n + CH]) for n in range(4)
        )
        lane = lax.broadcasted_iota(jnp.int32, (1, 4 * TOK), 1) % (2 * TOK)
        drop = jnp.where(flag > 0, 0.0, NEG).astype(F32)
        self.bias0 = jnp.where(lane < TOK, 0.0, drop)
        self.bias1 = jnp.where(lane < TOK, drop, 0.0)
        self.d_q = [None] * HEADS
        self.d_k = [None] * HEADS
        self.d_v = [None] * HEADS

    def products(self, pair):
        return pair_product(self.k, self.q_t, pair), pair_product(self.v, self.a_t, pair)

    def soften(self, scores, d_prob):
        top = jnp.max(scores[:TOK], axis=0, keepdims=True) + self.bias0
        low = jnp.max(scores[TOK:], axis=0, keepdims=True) + self.bias1
        peak = jnp.maximum(top, low)
        weight = cat(
            [
                jnp.exp2(scores[:TOK] - (peak - self.bias0)),
                jnp.exp2(scores[TOK:] - (peak - self.bias1)),
            ],
            0,
        )
        prob = weight * (1.0 / jnp.sum(weight, axis=0, keepdims=True))
        term = prob * d_prob
        d_score = term - prob * jnp.sum(term, axis=0, keepdims=True)
        return split(prob), split(d_score)

    def gather(self, pair, prob, d_score):
        for j in range(2):
            head = 2 * pair + j
            rows = slice(HEAD * head, HEAD * head + HEAD)
            cols = slice(2 * TOK * j, 2 * TOK * j + 2 * TOK)
            left = cat([self.k_t[0][rows], self.k_t[1][rows]], 0)
            both = mm(cat([left, left], 1), cat([d_score[0][:, cols], d_score[1][:, cols]], 0))
            self.d_q[head] = both[:HEAD] + both[HEAD:]
            lane = lax.broadcasted_iota(jnp.int32, (2 * TOK, CH), 1)
            own = (lane >= HEAD * head) & (lane < HEAD * head + HEAD)

            def masked(value):
                part = cat([jnp.where(own, half, jnp.zeros_like(half)) for half in value], 1)
                return cat([part, part], 0)

            self.d_v[head] = mm(cat([prob[0][:, cols], prob[1][:, cols]], 1), masked(self.a))
            self.d_k[head] = mm(cat([d_score[0][:, cols], d_score[1][:, cols]], 1), masked(self.q))

    def finish(self, w_back):
        d_q = (cat(self.d_q, 0) * SCALE).T
        d_k = self.d_k[0] + self.d_k[1] + self.d_k[2] + self.d_k[3]
        d_v = self.d_v[0] + self.d_v[1] + self.d_v[2] + self.d_v[3]
        d_k = (d_k[:, :CH] + d_k[:, CH:]) * SCALE
        d_v = d_v[:, :CH] + d_v[:, CH:]
        halves = split(d_q) + split(d_k) + split(d_v)
        return mm(cat(list(halves), 1), w_back)


def window_group(feats, grads, flags, w_across, w_along, w_back):
    both = cat([cat(feats, 0), cat(grads, 0)], 1)
    across = mm_nt(w_across, both)
    along = mm(both, w_along)
    windows = []
    for n, flag in enumerate(flags):
        part = slice(2 * TOK * n, 2 * TOK * n + 2 * TOK)
        windows.append(Window(across[:, part], along[part], flag))
    units = [(window, pair) for window in windows for pair in range(HEADS // 2)]
    ready, soft = {}, {}
    ready[0] = units[0][0].products(units[0][1])
    for n in range(len(units)):
        if n + 1 < len(units):
            ready[n + 1] = units[n + 1][0].products(units[n + 1][1])
        soft[n] = units[n][0].soften(*ready.pop(n))
        if n >= 1:
            units[n - 1][0].gather(units[n - 1][1], *soft.pop(n - 1))
    units[-1][0].gather(units[-1][1], *soft.pop(len(units) - 1))
    return [window.finish(w_back) for window in windows]


def run_group(first, total, picks, feat, grad, result, weights):
    feats, grads, flags, spots = [], [], [], []
    for n in range(GROUP):
        pick = picks[jnp.minimum(first + n, total - 1)]
        row = pick // 512
        col = (pick // 2) % 256
        feats.append(feat[:, pl.ds(row, WIN), pl.ds(col, WIN), :].reshape(2 * TOK, CH).astype(BF16))
        grads.append(grad[:, pl.ds(row, WIN), pl.ds(col, WIN), :].reshape(2 * TOK, CH).astype(BF16))
        flags.append(pick % 2)
        spots.append((row, col))
    outs = window_group(feats, grads, flags, *(w[...] for w in weights))
    for (row, col), out in zip(spots, outs):
        result[:, pl.ds(row, WIN), pl.ds(col, WIN), :] = out.reshape(2, WIN, WIN, CH)


def inner_kernel(
    code, feat_hbm, grad_hbm, w_across, w_along, w_back, out_hbm,
    feat_in, grad_in, feat, grad, result, picks, upto, in_sem, out_sem,
):
    chunks = feat.shape[1] // WIN
    across = feat.shape[2] // WIN

    def load(c, hbm, buf, which):
        rows = pl.ds(c * WIN, WIN)
        return pltpu.make_async_copy(hbm.at[:, rows], buf.at[:, rows], in_sem.at[c, which])

    def store(s):
        rows = pl.ds(s * WIN + HALF, WIN)
        return pltpu.make_async_copy(result.at[:, rows], out_hbm.at[:, rows], out_sem.at[s])

    @pl.loop(0, chunks)
    def _(c):
        load(c, feat_hbm, feat_in, 0).start()
        load(c, grad_hbm, grad_in, 1).start()

    def scan(t, count):
        a = t // across
        b = t % across
        value = code[a, b]
        live = (value >= 0) & (a < chunks - 1) & (b < across - 1)
        picks[count] = ((a * WIN + HALF) * 256 + b * WIN + HALF) * 2 + value
        count = count + live.astype(jnp.int32)
        upto[a] = count
        return count

    total = lax.fori_loop(0, chunks * across, scan, jnp.int32(0))

    @pl.loop(0, chunks)
    def _(c):
        rows = pl.ds(c * WIN, WIN)
        result[:, rows] = jnp.zeros((2, WIN) + result.shape[2:], F32)

    def step(c, carry):
        done, stored = carry
        load(c, feat_hbm, feat_in, 0).wait()
        load(c, grad_hbm, grad_in, 1).wait()
        rows = pl.ds(c * WIN, WIN)
        feat[:, rows] = feat_in[:, rows].astype(F32)
        grad[:, rows] = grad_in[:, rows].astype(F32)
        ready = jnp.where(c > 0, upto[jnp.maximum(c - 1, 0)], 0)
        last = c == chunks - 1
        groups = (ready - done + jnp.where(last, GROUP - 1, 0)) // GROUP

        @pl.loop(0, groups)
        def _(n):
            run_group(done + n * GROUP, total, picks, feat, grad, result, (w_across, w_along, w_back))

        done = done + groups * GROUP

        def put(s, stored):
            full = (s == stored) & (s < c) & (upto[s] <= done)

            @pl.when(full)
            def _():
                store(s).start()

            return stored + full.astype(jnp.int32)

        return done, lax.fori_loop(0, chunks - 1, put, stored)

    lax.fori_loop(0, chunks, step, (jnp.int32(0), jnp.int32(0)))

    @pl.loop(0, chunks - 1)
    def _(s):
        store(s).wait()


def inner_windows(code, features, grad_out, weights):
    shape = features.shape
    chunks = shape[1] // WIN
    hbm = pl.BlockSpec(memory_space=pl.ANY)
    vmem = pl.BlockSpec(memory_space=pltpu.VMEM)
    smem = pl.BlockSpec(memory_space=pltpu.SMEM)
    return pl.pallas_call(
        inner_kernel,
        out_shape=jax.ShapeDtypeStruct(shape, F32),
        in_specs=[smem, hbm, hbm, vmem, vmem, vmem],
        out_specs=hbm,
        scratch_shapes=[
            pltpu.VMEM(shape, BF16),
            pltpu.VMEM(shape, BF16),
            pltpu.VMEM(shape, F32),
            pltpu.VMEM(shape, F32),
            pltpu.VMEM(shape, F32),
            pltpu.SMEM((chunks * (shape[2] // WIN) + 1,), jnp.int32),
            pltpu.SMEM((chunks,), jnp.int32),
            pltpu.SemaphoreType.DMA((chunks, 2)),
            pltpu.SemaphoreType.DMA((chunks - 1,)),
        ],
        compiler_params=pltpu.CompilerParams(vmem_limit_bytes=48 * 2**20),
        cost_estimate=pl.CostEstimate(flops=105 * 235 * 10**6, bytes_accessed=16 * 2**20, transcendentals=105 * 65536),
        name="inner_windows",
    )(code, features, grad_out, *weights)


def edge_kernel(
    code, code_above, code_left, code_corner,
    feat_hbm, grad_hbm, above, below, left, right, c_al, c_ar, c_bl, c_br,
    w_across, w_along, w_back, before, out_hbm,
    rows_in, cols_in, feat, grad, result, sides, picks, in_sem, side_sem, out_sem,
):
    rows, cols = feat_hbm.shape[1], feat_hbm.shape[2]
    down, wide = rows // WIN + 1, cols // WIN + 1
    inner = rows - 2 * HALF
    copies = []
    for n, hbm in enumerate((feat_hbm, grad_hbm)):
        for m, at in enumerate((0, rows - HALF)):
            copies.append(pltpu.make_async_copy(hbm.at[:, pl.ds(at, HALF)], rows_in.at[n, m], in_sem.at[n, m]))
        for m, at in enumerate((0, cols - 16)):
            copies.append(
                pltpu.make_async_copy(
                    hbm.at[:, pl.ds(HALF, inner), pl.ds(at, 16)], cols_in.at[n, m], in_sem.at[n, 2 + m]
                )
            )
    for copy in copies:
        copy.start()
    side_at = (0, cols - WIN)
    side_in = [
        pltpu.make_async_copy(
            before.at[:, pl.ds(HALF, inner), pl.ds(at, WIN)], sides.at[m], side_sem.at[m]
        )
        for m, at in enumerate(side_at)
    ]
    for copy in side_in:
        copy.start()

    def scan(t, count):
        a = t // wide
        b = t % wide
        edge = (a == 0) | (a == down - 1) | (b == 0) | (b == wide - 1)
        a1 = jnp.maximum(a - 1, 0)
        b1 = jnp.maximum(b - 1, 0)
        own = code[a1, b1]
        up = code_above[down - 2, b1]
        beside = code_left[a1, wide - 2]
        corner = code_corner[down - 2, wide - 2]
        value = jnp.where(a > 0, jnp.where(b > 0, own, beside), jnp.where(b > 0, up, corner))
        picks[count] = (a * WIN * 256 + b * WIN + HALF) * 2 + value
        return count + (edge & (value >= 0)).astype(jnp.int32)

    total = lax.fori_loop(0, down * wide, scan, jnp.int32(0))

    for at in (0, rows):
        result[:, at : at + WIN] = jnp.zeros((2, WIN) + result.shape[2:], F32)
    for at in (0, cols):
        result[:, WIN:rows, at : at + 2 * WIN] = jnp.zeros((2, rows - WIN, 2 * WIN, CH), F32)

    for n, frame in enumerate((feat, grad)):
        frame[:, :HALF, WIN : WIN + cols] = above[n].astype(F32)
        frame[:, rows + HALF :, WIN : WIN + cols] = below[n].astype(F32)
        frame[:, HALF : rows + HALF, :WIN] = left[n].astype(F32)
        frame[:, HALF : rows + HALF, WIN + cols :] = right[n].astype(F32)
        frame[:, :HALF, :WIN] = c_al[n].astype(F32)
        frame[:, :HALF, WIN + cols :] = c_ar[n].astype(F32)
        frame[:, rows + HALF :, :WIN] = c_bl[n].astype(F32)
        frame[:, rows + HALF :, WIN + cols :] = c_br[n].astype(F32)
    for copy in copies:
        copy.wait()
    for n, frame in enumerate((feat, grad)):
        frame[:, HALF : 2 * HALF, WIN : WIN + cols] = rows_in[n, 0].astype(F32)
        frame[:, rows : rows + HALF, WIN : WIN + cols] = rows_in[n, 1].astype(F32)
        frame[:, 2 * HALF : rows, WIN : WIN + 16] = cols_in[n, 0].astype(F32)
        frame[:, 2 * HALF : rows, cols - WIN : cols + WIN] = cols_in[n, 1].astype(F32)

    @pl.loop(0, (total + GROUP - 1) // GROUP)
    def _(n):
        run_group(n * GROUP, total, picks, feat, grad, result, (w_across, w_along, w_back))

    back = [
        pltpu.make_async_copy(
            result.at[:, pl.ds(HALF, HALF), pl.ds(WIN, cols)], out_hbm.at[:, pl.ds(0, HALF)], out_sem.at[0]
        ),
        pltpu.make_async_copy(
            result.at[:, pl.ds(rows, HALF), pl.ds(WIN, cols)], out_hbm.at[:, pl.ds(rows - HALF, HALF)], out_sem.at[1]
        ),
    ]
    for m, at in enumerate(side_at):
        side_in[m].wait()
        first = 0 if m == 0 else HALF
        sides[m, :, :, first : first + HALF] = result[:, WIN:rows, WIN + at + first : WIN + at + first + HALF]
        back.append(
            pltpu.make_async_copy(
                sides.at[m], out_hbm.at[:, pl.ds(HALF, inner), pl.ds(at, WIN)], out_sem.at[2 + m]
            )
        )
    for copy in back:
        copy.start()
    for copy in back:
        copy.wait()


def edge_windows(codes, features, grad_out, halos, weights, before):
    shape = features.shape
    rows, cols = shape[1], shape[2]
    frame = (2, rows + 2 * HALF, cols + 2 * WIN, CH)
    hbm = pl.BlockSpec(memory_space=pl.ANY)
    vmem = pl.BlockSpec(memory_space=pltpu.VMEM)
    smem = pl.BlockSpec(memory_space=pltpu.SMEM)
    operands = (*codes, features, grad_out, *halos, *weights, before)
    return pl.pallas_call(
        edge_kernel,
        out_shape=jax.ShapeDtypeStruct(shape, F32),
        in_specs=[smem] * 4 + [hbm] * 2 + [vmem] * 11 + [hbm],
        out_specs=hbm,
        scratch_shapes=[
            pltpu.VMEM((2, 2, 2, HALF, cols, CH), BF16),
            pltpu.VMEM((2, 2, 2, rows - 2 * HALF, 16, CH), BF16),
            pltpu.VMEM(frame, F32),
            pltpu.VMEM(frame, F32),
            pltpu.VMEM(frame, F32),
            pltpu.VMEM((2, 2, rows - 2 * HALF, WIN, CH), F32),
            pltpu.SMEM(((rows // WIN + 1) * (cols // WIN + 1) + 1,), jnp.int32),
            pltpu.SemaphoreType.DMA((2, 4)),
            pltpu.SemaphoreType.DMA((2,)),
            pltpu.SemaphoreType.DMA((4,)),
        ],
        input_output_aliases={len(operands) - 1: 0},
        compiler_params=pltpu.CompilerParams(vmem_limit_bytes=56 * 2**20),
        cost_estimate=pl.CostEstimate(flops=48 * 235 * 10**6, bytes_accessed=8 * 2**20, transcendentals=48 * 65536),
        name="edge_windows",
    )(*operands)


def moved(value, down, right):
    height, width = lax.axis_size("row"), lax.axis_size("col")
    pairs = [
        (i * width + j, ((i + down) % height) * width + (j + right) % width)
        for i in range(height)
        for j in range(width)
    ]
    return lax.ppermute(value, ("row", "col"), pairs)


def on_device(features, grad_out, w_qkv, w_out, cross_live, route):
    def both(rows, cols):
        return jnp.stack([features[:, rows, cols], grad_out[:, rows, cols]])

    full, first, last = slice(None), slice(None, HALF), slice(-HALF, None)
    west, east = slice(None, WIN), slice(-WIN, None)
    halos = [
        moved(both(last, full), 1, 0),
        moved(both(first, full), -1, 0),
        moved(both(full, east), 0, 1),
        moved(both(full, west), 0, -1),
        moved(both(last, east), 1, 1),
        moved(both(last, west), 1, -1),
        moved(both(first, east), -1, 1),
        moved(both(first, west), -1, -1),
    ]
    ids = jnp.arange(cross_live.size, dtype=jnp.int32).reshape(cross_live.shape)
    live = jnp.any(route.reshape(1, 1, -1) == ids[:, :, None], axis=-1)
    code = jnp.where(live, (cross_live > 0).astype(jnp.int32), -1)
    codes = [code, moved(code, 1, 0), moved(code, 0, 1), moved(code, 1, 1)]

    def zeros(height, width):
        return jnp.zeros((height, width), BF16)

    w_across = cat(
        [cat([w_qkv[:, : 2 * CH].T, zeros(2 * CH, CH)], 1), cat([zeros(CH, CH), w_out], 1)], 0
    )
    w_along = cat(
        [
            cat([w_qkv[:, CH:], w_qkv[:, :CH], zeros(CH, CH)], 1),
            cat([zeros(CH, 3 * CH), w_out.T], 1),
        ],
        0,
    )
    back = [w_qkv[:, CH * n : CH * n + CH].T for n in range(3)]
    w_back = cat([back[0], back[0], back[1], back[1], back[2], back[2]], 0)
    weights = (w_across, w_along, w_back)
    inner = inner_windows(code, features, grad_out, weights)
    return edge_windows(codes, features, grad_out, halos, weights, inner)


def solution(mesh):
    return jax.shard_map(
        on_device,
        mesh=mesh,
        in_specs=(
            P(None, "row", "col", None),
            P(None, "row", "col", None),
            P(),
            P(),
            P("row", "col"),
            P("row", "col", None, None),
        ),
        out_specs=P(None, "row", "col", None),
        check_vma=False,
    )
```

```python
import functools
import math

import jax
import jax.numpy as jnp
from jax import lax
from jax.experimental import pallas as pl
from jax.experimental.pallas import tpu as pltpu
from jax.sharding import PartitionSpec as P

F32 = jnp.float32
BF16 = jnp.bfloat16
HEADS = 4
WIN = 8
HALF = 4
CH = 128
HEAD = CH // HEADS
TOK = WIN * WIN
GROUP = 4
NEG = -1e30
LOG2E = math.log2(math.e)
SCALE = 1.0 / math.sqrt(HEAD)


def split(value):
    high = value.astype(BF16)
    return high, (value - high.astype(F32)).astype(BF16)


def mm(a, b):
    return lax.dot_general(a, b, (((1,), (0,)), ((), ())), preferred_element_type=F32)


def mm_nt(a, b):
    return lax.dot_general(a, b, (((1,), (1,)), ((), ())), preferred_element_type=F32)


def cat(parts, axis):
    return jnp.concatenate(parts, axis=axis)


def head_pair_rows(high, low, pair):
    zero = jnp.zeros((HEAD, 2 * TOK), BF16)
    zeros = jnp.zeros((2 * HEAD, 4 * TOK), BF16)
    first, second = (slice(HEAD * h, HEAD * h + HEAD) for h in (2 * pair, 2 * pair + 1))
    top = [cat([high[first], zero], 1), cat([zero, high[second]], 1)]
    fix = [cat([low[first], zero], 1), cat([zero, low[second]], 1)]
    tail = fix + [zeros] if pair == 0 else [zeros] + fix
    return cat(top + top + tail, 0)


def pair_product(tokens, columns, pair):
    lanes = slice(2 * HEAD * pair, 2 * HEAD * pair + 2 * HEAD)
    left = cat([tokens[0][:, lanes], tokens[1][:, lanes], tokens[0]], 1)
    return mm(left, head_pair_rows(columns[0], columns[1], pair))


def across_parts(across):
    return [split(across[CH * n : CH * n + CH]) for n in range(3)]


def project(window_feats, window_grads, weights):
    w_across, w_along = weights[0][...], weights[1][...]
    feats = cat(window_feats, 0)
    across = mm_nt(w_across, cat([feats, cat(window_grads, 0)], 1))
    along = mm(cat([feats, feats], 1), w_along)
    out = []
    for n in range(len(window_feats)):
        part = slice(2 * TOK * n, 2 * TOK * n + 2 * TOK)
        out.append(
            across_parts(across[:, part]) + [split(along[part, :CH]), split(along[part, CH:])]
        )
    return out


def products(parts, pair):
    query, _, cotangent, keys, values = parts
    return pair_product(keys, query, pair), pair_product(values, cotangent, pair)


def soften(flag, scores, d_prob):
    lane = lax.broadcasted_iota(jnp.int32, (1, 4 * TOK), 1) % (2 * TOK)
    drop = jnp.where(flag > 0, 0.0, NEG).astype(F32)
    bias0 = jnp.where(lane < TOK, 0.0, drop)
    bias1 = jnp.where(lane < TOK, drop, 0.0)
    peak = jnp.maximum(
        jnp.max(scores[:TOK], axis=0, keepdims=True) + bias0,
        jnp.max(scores[TOK:], axis=0, keepdims=True) + bias1,
    )
    weight = cat(
        [jnp.exp2(scores[:TOK] - (peak - bias0)), jnp.exp2(scores[TOK:] - (peak - bias1))], 0
    )
    prob = weight * (1.0 / jnp.sum(weight, axis=0, keepdims=True))
    term = prob * d_prob
    d_score = term - prob * jnp.sum(term, axis=0, keepdims=True)
    prob, d_score = split(prob), split(d_score)
    out = []
    for j in range(2):
        cols = slice(2 * TOK * j, 2 * TOK * j + 2 * TOK)
        out.append(
            (
                cat([d_score[0][:, cols], d_score[1][:, cols]], 0),
                cat([prob[0][:, cols].T, prob[1][:, cols].T], 0),
                cat([d_score[0][:, cols].T, d_score[1][:, cols].T], 0),
            )
        )
    return out


def gather(sides, soft):
    out = [[], [], []]
    for j in range(2):
        rows = slice(HEAD * j, HEAD * j + HEAD)
        by_key, prob, by_query = soft[j]
        for n, (side, right) in enumerate(
            ((sides[1], by_key), (sides[0], by_query), (sides[2], prob))
        ):
            left = cat([side[0][rows], side[1][rows]], 0)
            both = mm(cat([left, left], 1), right)
            out[n].append(both[:HEAD] + both[HEAD:])
    return [cat(part, 0) for part in out]


def pair_sides(parts, pair):
    rows = slice(2 * HEAD * pair, 2 * HEAD * pair + 2 * HEAD)
    return [(part[0][rows], part[1][rows]) for part in parts[:3]]


def finish(grads, w_back):
    whole = cat([cat([g[p][n] for n in range(3) for p in range(2)], 0) for g in grads], 1)
    out = mm(w_back[...], cat(split(whole), 0))
    return [out[:, 2 * TOK * n : 2 * TOK * n + 2 * TOK].T for n in range(len(grads))]


STASH = [
    pltpu.VMEM((2, 10, CH, 2 * TOK), BF16),
    pltpu.VMEM((2, 2 * TOK, 4 * TOK), F32),
    pltpu.VMEM((2, 3, 4 * TOK, 2 * TOK), BF16),
    pltpu.VMEM((6, 2 * HEAD, 2 * TOK), BF16),
    pltpu.VMEM((3, 3, 2 * HEAD, 2 * TOK), F32),
]


def run_windows(total, picks, feat, grad, result, weights, stash, before, after):
    ahead, scored, softened, sided, kept = stash
    groups = (total + GROUP - 1) // GROUP

    def place(n):
        pick = picks[jnp.clip(n, 0, total - 1)]
        return pick // 512, (pick // 2) % 256, pick % 2

    def window(ref, n):
        row, col, _ = place(n)
        value = ref[:, pl.ds(row, WIN), pl.ds(col, WIN), :]
        return value.reshape(2 * TOK, CH).astype(BF16)

    def projected(n):
        return project(
            [window(feat, n), window(feat, n + 1)], [window(grad, n), window(grad, n + 1)], weights
        )

    def put(n, value):
        row, col, _ = place(n)
        result[:, pl.ds(row, WIN), pl.ds(col, WIN), :] = value.reshape(2, WIN, WIN, CH)

    def stash_ahead(parts):
        for w in range(2):
            for n in range(5):
                for half in range(2):
                    ahead[w, 2 * n + half] = parts[w][n][half]
        scored[0], scored[1] = products(parts[0], 0)

    def close(first):
        soft = [tuple(softened[j, n] for n in range(3)) for j in range(2)]
        last = gather([(sided[2 * n], sided[2 * n + 1]) for n in range(3)], soft)
        held = [[kept[u, n] for n in range(3)] for u in range(3)]
        for n, value in enumerate(finish([held[:2], [held[2], last]], weights[2])):
            put(first - 2 + n, value)

    @pl.when(total > 0)
    def _():
        before(1)
        stash_ahead(projected(0))

    @pl.loop(0, groups)
    def _(i):
        first = i * GROUP
        before(first + GROUP + 1)
        parts = [
            [(ahead[w, 2 * n], ahead[w, 2 * n + 1]) for n in range(5)] for w in range(2)
        ] + [None, None]
        flags = [place(first + n)[2] for n in range(GROUP)]
        ready = {0: (scored[0], scored[1])}
        soft, done = {}, {}
        for u in range(2 * GROUP):
            if u < 2 * GROUP - 1:
                ready[u + 1] = products(parts[(u + 1) // 2], (u + 1) % 2)
            else:
                stash_ahead(following)
            soft[u] = soften(flags[u // 2], *ready.pop(u))
            if u == 0:
                close(first)
                parts[2:] = projected(first + 2)
            else:
                v = u - 1
                done[v] = gather(pair_sides(parts[v // 2], v % 2), soft.pop(v))
            if u == 4:
                outs = finish([[done[0], done[1]], [done[2], done[3]]], weights[2])
                for n, value in enumerate(outs):
                    put(first + n, value)
            if u == 5:
                following = projected(first + GROUP)
        end = soft.pop(2 * GROUP - 1)
        for j in range(2):
            for n in range(3):
                softened[j, n] = end[j][n]
        for n, side in enumerate(pair_sides(parts[-1], 1)):
            sided[2 * n], sided[2 * n + 1] = side
        for n, u in enumerate((4, 5, 6)):
            for m in range(3):
                kept[n, m] = done[u][m]
        after(first + 2)

    @pl.when(total > 0)
    def _():
        close(groups * GROUP)


def inner_kernel(
    code, feat_hbm, grad_hbm, w_across, w_along, w_back, out_hbm,
    feat_in, grad_in, feat, grad, result, picks, upto, marks, in_sem, out_sem, *stash,
):
    chunks = feat.shape[1] // WIN
    across = feat.shape[2] // WIN

    def load(c, hbm, buf, which):
        rows = pl.ds(c * WIN, WIN)
        return pltpu.make_async_copy(hbm.at[:, rows], buf.at[:, rows], in_sem.at[c, which])

    def store(s):
        rows = pl.ds(s * WIN + HALF, WIN)
        return pltpu.make_async_copy(result.at[:, rows], out_hbm.at[:, rows], out_sem.at[s])

    @pl.loop(0, chunks)
    def _(c):
        load(c, feat_hbm, feat_in, 0).start()
        load(c, grad_hbm, grad_in, 1).start()

    def scan(t, count):
        a = t // across
        b = t % across
        value = code[a, b]
        live = (value >= 0) & (a < chunks - 1) & (b < across - 1)
        picks[count] = ((a * WIN + HALF) * 256 + b * WIN + HALF) * 2 + value
        count = count + live.astype(jnp.int32)
        upto[a] = count
        return count

    total = lax.fori_loop(0, chunks * across, scan, jnp.int32(0))

    @pl.loop(0, chunks)
    def _(c):
        rows = pl.ds(c * WIN, WIN)
        result[:, rows] = jnp.zeros((2, WIN) + result.shape[2:], F32)

    marks[0] = 0
    marks[1] = 0

    def convert(until):
        @pl.loop(marks[0], until)
        def _(c):
            load(c, feat_hbm, feat_in, 0).wait()
            load(c, grad_hbm, grad_in, 1).wait()
            rows = pl.ds(c * WIN, WIN)
            feat[:, rows] = feat_in[:, rows].astype(F32)
            grad[:, rows] = grad_in[:, rows].astype(F32)

        marks[0] = jnp.maximum(marks[0], until)

    def before(n):
        row = picks[jnp.minimum(n, total - 1)] // 512
        convert((row + WIN - 1) // WIN + 1)

    def after(count):
        def put(s, stored):
            full = (s == stored) & (upto[s] <= jnp.minimum(count, total - 1))

            @pl.when(full)
            def _():
                store(s).start()

            return stored + full.astype(jnp.int32)

        marks[1] = lax.fori_loop(marks[1], chunks - 1, put, marks[1])

    run_windows(total, picks, feat, grad, result, (w_across, w_along, w_back), stash, before, after)
    convert(chunks)

    @pl.loop(marks[1], chunks - 1)
    def _(s):
        store(s).start()

    @pl.loop(0, chunks - 1)
    def _(s):
        store(s).wait()


def inner_windows(code, features, grad_out, weights):
    shape = features.shape
    chunks = shape[1] // WIN
    hbm = pl.BlockSpec(memory_space=pl.ANY)
    vmem = pl.BlockSpec(memory_space=pltpu.VMEM)
    smem = pl.BlockSpec(memory_space=pltpu.SMEM)
    return pl.pallas_call(
        inner_kernel,
        out_shape=jax.ShapeDtypeStruct(shape, F32),
        in_specs=[smem, hbm, hbm, vmem, vmem, vmem],
        out_specs=hbm,
        scratch_shapes=[
            pltpu.VMEM(shape, BF16),
            pltpu.VMEM(shape, BF16),
            pltpu.VMEM(shape, F32),
            pltpu.VMEM(shape, F32),
            pltpu.VMEM(shape, F32),
            pltpu.SMEM((chunks * (shape[2] // WIN) + 1,), jnp.int32),
            pltpu.SMEM((chunks,), jnp.int32),
            pltpu.SMEM((2,), jnp.int32),
            pltpu.SemaphoreType.DMA((chunks, 2)),
            pltpu.SemaphoreType.DMA((chunks - 1,)),
            *STASH,
        ],
        compiler_params=pltpu.CompilerParams(vmem_limit_bytes=48 * 2**20),
        cost_estimate=pl.CostEstimate(flops=105 * 235 * 10**6, bytes_accessed=16 * 2**20, transcendentals=105 * 65536),
        name="inner_windows",
    )(code, features, grad_out, *weights)


def edge_kernel(
    code, code_above, code_left, code_corner,
    feat_hbm, grad_hbm, above, below, left, right, c_al, c_ar, c_bl, c_br,
    w_across, w_along, w_back, before, out_hbm,
    rows_in, cols_in, feat, grad, result, sides, picks, in_sem, side_sem, out_sem, *stash,
):
    rows, cols = feat_hbm.shape[1], feat_hbm.shape[2]
    down, wide = rows // WIN + 1, cols // WIN + 1
    inner = rows - 2 * HALF
    copies = []
    for n, hbm in enumerate((feat_hbm, grad_hbm)):
        for m, at in enumerate((0, rows - HALF)):
            copies.append(pltpu.make_async_copy(hbm.at[:, pl.ds(at, HALF)], rows_in.at[n, m], in_sem.at[n, m]))
        for m, at in enumerate((0, cols - 16)):
            copies.append(
                pltpu.make_async_copy(
                    hbm.at[:, pl.ds(HALF, inner), pl.ds(at, 16)], cols_in.at[n, m], in_sem.at[n, 2 + m]
                )
            )
    for copy in copies:
        copy.start()
    side_at = (0, cols - WIN)
    side_in = [
        pltpu.make_async_copy(
            before.at[:, pl.ds(HALF, inner), pl.ds(at, WIN)], sides.at[m], side_sem.at[m]
        )
        for m, at in enumerate(side_at)
    ]
    for copy in side_in:
        copy.start()

    def scan(t, count):
        a = t // wide
        b = t % wide
        edge = (a == 0) | (a == down - 1) | (b == 0) | (b == wide - 1)
        a1 = jnp.maximum(a - 1, 0)
        b1 = jnp.maximum(b - 1, 0)
        own = code[a1, b1]
        up = code_above[down - 2, b1]
        beside = code_left[a1, wide - 2]
        corner = code_corner[down - 2, wide - 2]
        value = jnp.where(a > 0, jnp.where(b > 0, own, beside), jnp.where(b > 0, up, corner))
        picks[count] = (a * WIN * 256 + b * WIN + HALF) * 2 + value
        return count + (edge & (value >= 0)).astype(jnp.int32)

    total = lax.fori_loop(0, down * wide, scan, jnp.int32(0))

    for at in (0, rows):
        result[:, at : at + WIN] = jnp.zeros((2, WIN) + result.shape[2:], F32)
    for at in (0, cols):
        result[:, WIN:rows, at : at + 2 * WIN] = jnp.zeros((2, rows - WIN, 2 * WIN, CH), F32)

    for n, frame in enumerate((feat, grad)):
        frame[:, :HALF, WIN : WIN + cols] = above[n].astype(F32)
        frame[:, rows + HALF :, WIN : WIN + cols] = below[n].astype(F32)
        frame[:, HALF : rows + HALF, :WIN] = left[n].astype(F32)
        frame[:, HALF : rows + HALF, WIN + cols :] = right[n].astype(F32)
        frame[:, :HALF, :WIN] = c_al[n].astype(F32)
        frame[:, :HALF, WIN + cols :] = c_ar[n].astype(F32)
        frame[:, rows + HALF :, :WIN] = c_bl[n].astype(F32)
        frame[:, rows + HALF :, WIN + cols :] = c_br[n].astype(F32)
    for copy in copies:
        copy.wait()
    for n, frame in enumerate((feat, grad)):
        frame[:, HALF : 2 * HALF, WIN : WIN + cols] = rows_in[n, 0].astype(F32)
        frame[:, rows : rows + HALF, WIN : WIN + cols] = rows_in[n, 1].astype(F32)
        frame[:, 2 * HALF : rows, WIN : WIN + 16] = cols_in[n, 0].astype(F32)
        frame[:, 2 * HALF : rows, cols - WIN : cols + WIN] = cols_in[n, 1].astype(F32)

    run_windows(
        total, picks, feat, grad, result, (w_across, w_along, w_back), stash,
        lambda n: None, lambda n: None,
    )

    back = [
        pltpu.make_async_copy(
            result.at[:, pl.ds(HALF, HALF), pl.ds(WIN, cols)], out_hbm.at[:, pl.ds(0, HALF)], out_sem.at[0]
        ),
        pltpu.make_async_copy(
            result.at[:, pl.ds(rows, HALF), pl.ds(WIN, cols)], out_hbm.at[:, pl.ds(rows - HALF, HALF)], out_sem.at[1]
        ),
    ]
    for m, at in enumerate(side_at):
        side_in[m].wait()
        first = 0 if m == 0 else HALF
        sides[m, :, :, first : first + HALF] = result[:, WIN:rows, WIN + at + first : WIN + at + first + HALF]
        back.append(
            pltpu.make_async_copy(
                sides.at[m], out_hbm.at[:, pl.ds(HALF, inner), pl.ds(at, WIN)], out_sem.at[2 + m]
            )
        )
    for copy in back:
        copy.start()
    for copy in back:
        copy.wait()


def edge_windows(codes, features, grad_out, halos, weights, before):
    shape = features.shape
    rows, cols = shape[1], shape[2]
    frame = (2, rows + 2 * HALF, cols + 2 * WIN, CH)
    hbm = pl.BlockSpec(memory_space=pl.ANY)
    vmem = pl.BlockSpec(memory_space=pltpu.VMEM)
    smem = pl.BlockSpec(memory_space=pltpu.SMEM)
    operands = (*codes, features, grad_out, *halos, *weights, before)
    return pl.pallas_call(
        edge_kernel,
        out_shape=jax.ShapeDtypeStruct(shape, F32),
        in_specs=[smem] * 4 + [hbm] * 2 + [vmem] * 11 + [hbm],
        out_specs=hbm,
        scratch_shapes=[
            pltpu.VMEM((2, 2, 2, HALF, cols, CH), BF16),
            pltpu.VMEM((2, 2, 2, rows - 2 * HALF, 16, CH), BF16),
            pltpu.VMEM(frame, F32),
            pltpu.VMEM(frame, F32),
            pltpu.VMEM(frame, F32),
            pltpu.VMEM((2, 2, rows - 2 * HALF, WIN, CH), F32),
            pltpu.SMEM(((rows // WIN + 1) * (cols // WIN + 1) + 1,), jnp.int32),
            pltpu.SemaphoreType.DMA((2, 4)),
            pltpu.SemaphoreType.DMA((2,)),
            pltpu.SemaphoreType.DMA((4,)),
            *STASH,
        ],
        input_output_aliases={len(operands) - 1: 0},
        compiler_params=pltpu.CompilerParams(vmem_limit_bytes=56 * 2**20),
        cost_estimate=pl.CostEstimate(flops=48 * 235 * 10**6, bytes_accessed=8 * 2**20, transcendentals=48 * 65536),
        name="edge_windows",
    )(*operands)


def moved(value, down, right):
    height, width = lax.axis_size("row"), lax.axis_size("col")
    pairs = [
        (i * width + j, ((i + down) % height) * width + (j + right) % width)
        for i in range(height)
        for j in range(width)
    ]
    return lax.ppermute(value, ("row", "col"), pairs)


def weight_forms(w_qkv, w_out):
    def zeros(height, width):
        return jnp.zeros((height, width), BF16)

    w_across = cat(
        [cat([w_qkv[:, : 2 * CH].T, zeros(2 * CH, CH)], 1), cat([zeros(CH, CH), w_out], 1)], 0
    )
    scaled = w_qkv[:, CH:].astype(F32) * cat(
        [jnp.full((CH,), LOG2E * SCALE, F32), jnp.full((CH,), SCALE, F32)], 0
    )
    low = scaled - lax.reduce_precision(scaled, 8, 7)
    w_along = cat([scaled.astype(BF16), low.astype(BF16)], 0)
    w_back = cat([w_qkv, w_qkv], 1)
    return w_across, w_along, w_back


def on_device(features, grad_out, w_qkv, w_out, cross_live, route):
    def both(rows, cols):
        return jnp.stack([features[:, rows, cols], grad_out[:, rows, cols]])

    full, first, last = slice(None), slice(None, HALF), slice(-HALF, None)
    west, east = slice(None, WIN), slice(-WIN, None)
    halos = [
        moved(both(last, full), 1, 0),
        moved(both(first, full), -1, 0),
        moved(both(full, east), 0, 1),
        moved(both(full, west), 0, -1),
        moved(both(last, east), 1, 1),
        moved(both(last, west), 1, -1),
        moved(both(first, east), -1, 1),
        moved(both(first, west), -1, -1),
    ]
    ids = jnp.arange(cross_live.size, dtype=jnp.int32).reshape(cross_live.shape)
    live = jnp.any(route.reshape(1, 1, -1) == ids[:, :, None], axis=-1)
    code = jnp.where(live, (cross_live > 0).astype(jnp.int32), -1)
    codes = [code, moved(code, 1, 0), moved(code, 0, 1), moved(code, 1, 1)]

    weights = weight_forms(w_qkv, w_out)
    inner = inner_windows(code, features, grad_out, weights)
    return edge_windows(codes, features, grad_out, halos, weights, inner)


def solution(mesh):
    return jax.shard_map(
        on_device,
        mesh=mesh,
        in_specs=(
            P(None, "row", "col", None),
            P(None, "row", "col", None),
            P(),
            P(),
            P("row", "col"),
            P("row", "col", None, None),
        ),
        out_specs=P(None, "row", "col", None),
        check_vma=False,
    )
```

```python
import functools
import math

import jax
import jax.numpy as jnp
from jax import lax
from jax.experimental import pallas as pl
from jax.experimental.pallas import tpu as pltpu
from jax.sharding import PartitionSpec as P

F32 = jnp.float32
BF16 = jnp.bfloat16
HEADS = 4
WIN = 8
HALF = 4
CH = 128
HEAD = CH // HEADS
TOK = WIN * WIN
GROUP = 4
NEG = -1e30
LOG2E = math.log2(math.e)
SCALE = 1.0 / math.sqrt(HEAD)


def split(value):
    high = value.astype(BF16)
    return high, (value - high.astype(F32)).astype(BF16)


def mm(a, b):
    return lax.dot_general(a, b, (((1,), (0,)), ((), ())), preferred_element_type=F32)


def mm_nt(a, b):
    return lax.dot_general(a, b, (((1,), (1,)), ((), ())), preferred_element_type=F32)


def cat(parts, axis):
    return jnp.concatenate(parts, axis=axis)


def head_pair_rows(high, low, pair):
    zero = jnp.zeros((HEAD, 2 * TOK), BF16)
    zeros = jnp.zeros((2 * HEAD, 4 * TOK), BF16)
    first, second = (slice(HEAD * h, HEAD * h + HEAD) for h in (2 * pair, 2 * pair + 1))
    top = [cat([high[first], zero], 1), cat([zero, high[second]], 1)]
    fix = [cat([low[first], zero], 1), cat([zero, low[second]], 1)]
    tail = fix + [zeros] if pair == 0 else [zeros] + fix
    return cat(top + top + tail, 0)


def pair_product(tokens, columns, pair):
    lanes = slice(2 * HEAD * pair, 2 * HEAD * pair + 2 * HEAD)
    left = cat([tokens[0][:, lanes], tokens[1][:, lanes], tokens[0]], 1)
    return mm(left, head_pair_rows(columns[0], columns[1], pair))


def across_parts(across):
    return [split(across[CH * n : CH * n + CH]) for n in range(3)]


def project(window_feats, window_grads, weights):
    w_across, w_along = weights[0][...], weights[1][...]
    feats = cat(window_feats, 0)
    across = mm_nt(w_across, cat([feats, cat(window_grads, 0)], 1))
    along = mm(cat([feats, feats], 1), w_along)
    out = []
    for n in range(len(window_feats)):
        part = slice(2 * TOK * n, 2 * TOK * n + 2 * TOK)
        out.append(
            across_parts(across[:, part]) + [split(along[part, :CH]), split(along[part, CH:])]
        )
    return out


def products(parts, pair):
    query, _, cotangent, keys, values = parts
    return pair_product(keys, query, pair), pair_product(values, cotangent, pair)


def soften(flag, scores, d_prob):
    lane = lax.broadcasted_iota(jnp.int32, (1, 4 * TOK), 1) % (2 * TOK)
    drop = jnp.where(flag > 0, 0.0, NEG).astype(F32)
    bias0 = jnp.where(lane < TOK, 0.0, drop)
    bias1 = jnp.where(lane < TOK, drop, 0.0)
    peak = jnp.maximum(
        jnp.max(scores[:TOK], axis=0, keepdims=True) + bias0,
        jnp.max(scores[TOK:], axis=0, keepdims=True) + bias1,
    )
    weight = cat(
        [jnp.exp2(scores[:TOK] - (peak - bias0)), jnp.exp2(scores[TOK:] - (peak - bias1))], 0
    )
    prob = weight * (1.0 / jnp.sum(weight, axis=0, keepdims=True))
    term = prob * d_prob
    d_score = term - prob * jnp.sum(term, axis=0, keepdims=True)
    prob, d_score = split(prob), split(d_score)
    out = []
    for j in range(2):
        cols = slice(2 * TOK * j, 2 * TOK * j + 2 * TOK)
        out.append(
            (
                cat([d_score[0][:, cols], d_score[1][:, cols]], 0),
                cat([prob[0][:, cols].T, prob[1][:, cols].T], 0),
                cat([d_score[0][:, cols].T, d_score[1][:, cols].T], 0),
            )
        )
    return out


def gather(sides, soft):
    out = [[], [], []]
    for j in range(2):
        rows = slice(HEAD * j, HEAD * j + HEAD)
        by_key, prob, by_query = soft[j]
        for n, (side, right) in enumerate(
            ((sides[1], by_key), (sides[0], by_query), (sides[2], prob))
        ):
            left = cat([side[0][rows], side[1][rows]], 0)
            both = mm(cat([left, left], 1), right)
            out[n].append(both[:HEAD] + both[HEAD:])
    return [cat(part, 0) for part in out]


def pair_sides(parts, pair):
    rows = slice(2 * HEAD * pair, 2 * HEAD * pair + 2 * HEAD)
    return [(part[0][rows], part[1][rows]) for part in parts[:3]]


def finish(grads, w_back):
    whole = cat([cat([g[p][n] for n in range(3) for p in range(2)], 0) for g in grads], 1)
    out = mm(w_back[...], cat(split(whole), 0))
    return [out[:, 2 * TOK * n : 2 * TOK * n + 2 * TOK].T for n in range(len(grads))]


def weight_forms(w_qkv, w_out, w_across, w_along, w_back):
    zeros = jnp.zeros((CH, CH), BF16)
    for n in range(2):
        rows = slice(CH * n, CH * n + CH)
        w_across[rows, :CH] = w_qkv[:, rows].T
        w_across[rows, CH:] = zeros
    w_across[2 * CH :, :CH] = zeros
    w_across[2 * CH :, CH:] = w_out[...]
    for n, scale in enumerate((LOG2E * SCALE, SCALE)):
        cols = slice(CH * n, CH * n + CH)
        halves = split(w_qkv[:, CH + CH * n : 2 * CH + CH * n].astype(F32) * scale)
        for half in range(2):
            w_along[CH * half : CH * half + CH, cols] = halves[half]
    for half in range(2):
        w_back[:, 3 * CH * half : 3 * CH * half + 3 * CH] = w_qkv[...]


WEIGHTS = [
    pltpu.VMEM((3 * CH, 2 * CH), BF16),
    pltpu.VMEM((2 * CH, 2 * CH), BF16),
    pltpu.VMEM((CH, 6 * CH), BF16),
]


STASH = [
    pltpu.VMEM((2, 10, CH, 2 * TOK), BF16),
    pltpu.VMEM((2, 2 * TOK, 4 * TOK), F32),
    pltpu.VMEM((2, 3, 4 * TOK, 2 * TOK), BF16),
    pltpu.VMEM((6, 2 * HEAD, 2 * TOK), BF16),
    pltpu.VMEM((3, 3, 2 * HEAD, 2 * TOK), F32),
]


def run_windows(total, picks, feat, grad, result, weights, stash, before, after):
    ahead, scored, softened, sided, kept = stash
    groups = (total + GROUP - 1) // GROUP

    def place(n):
        pick = picks[jnp.clip(n, 0, total - 1)]
        return pick // 512, (pick // 2) % 256, pick % 2

    def window(ref, n):
        row, col, _ = place(n)
        value = ref[:, pl.ds(row, WIN), pl.ds(col, WIN), :]
        return value.reshape(2 * TOK, CH).astype(BF16)

    def projected(n):
        return project(
            [window(feat, n), window(feat, n + 1)], [window(grad, n), window(grad, n + 1)], weights
        )

    def put(n, value):
        row, col, _ = place(n)
        result[:, pl.ds(row, WIN), pl.ds(col, WIN), :] = value.reshape(2, WIN, WIN, CH)

    def stash_ahead(parts):
        for w in range(2):
            for n in range(5):
                for half in range(2):
                    ahead[w, 2 * n + half] = parts[w][n][half]
        scored[0], scored[1] = products(parts[0], 0)

    def close(first):
        soft = [tuple(softened[j, n] for n in range(3)) for j in range(2)]
        last = gather([(sided[2 * n], sided[2 * n + 1]) for n in range(3)], soft)
        held = [[kept[u, n] for n in range(3)] for u in range(3)]
        for n, value in enumerate(finish([held[:2], [held[2], last]], weights[2])):
            put(first - 2 + n, value)

    @pl.when(total > 0)
    def _():
        before(1)
        stash_ahead(projected(0))

    @pl.loop(0, groups)
    def _(i):
        first = i * GROUP
        before(first + GROUP + 1)
        parts = [
            [(ahead[w, 2 * n], ahead[w, 2 * n + 1]) for n in range(5)] for w in range(2)
        ] + [None, None]
        flags = [place(first + n)[2] for n in range(GROUP)]
        ready = {0: (scored[0], scored[1])}
        soft, done = {}, {}
        for u in range(2 * GROUP):
            if u < 2 * GROUP - 1:
                ready[u + 1] = products(parts[(u + 1) // 2], (u + 1) % 2)
            else:
                stash_ahead(following)
            soft[u] = soften(flags[u // 2], *ready.pop(u))
            if u == 0:
                close(first)
                parts[2:] = projected(first + 2)
            else:
                v = u - 1
                done[v] = gather(pair_sides(parts[v // 2], v % 2), soft.pop(v))
            if u == 4:
                outs = finish([[done[0], done[1]], [done[2], done[3]]], weights[2])
                for n, value in enumerate(outs):
                    put(first + n, value)
            if u == 5:
                following = projected(first + GROUP)
        end = soft.pop(2 * GROUP - 1)
        for j in range(2):
            for n in range(3):
                softened[j, n] = end[j][n]
        for n, side in enumerate(pair_sides(parts[-1], 1)):
            sided[2 * n], sided[2 * n + 1] = side
        for n, u in enumerate((4, 5, 6)):
            for m in range(3):
                kept[n, m] = done[u][m]
        after(first + 2)

    @pl.when(total > 0)
    def _():
        close(groups * GROUP)


def inner_kernel(
    code, feat_hbm, grad_hbm, w_qkv, w_out, out_hbm,
    feat_in, grad_in, feat, grad, result, picks, upto, marks, in_sem, out_sem, *held,
):
    weights, stash = held[:3], held[3:]
    chunks = feat.shape[1] // WIN
    across = feat.shape[2] // WIN

    def load(c, hbm, buf, which):
        rows = pl.ds(c * WIN, WIN)
        return pltpu.make_async_copy(hbm.at[:, rows], buf.at[:, rows], in_sem.at[c, which])

    def store(s):
        rows = pl.ds(s * WIN + HALF, WIN)
        return pltpu.make_async_copy(result.at[:, rows], out_hbm.at[:, rows], out_sem.at[s])

    @pl.loop(0, chunks)
    def _(c):
        load(c, feat_hbm, feat_in, 0).start()
        load(c, grad_hbm, grad_in, 1).start()

    weight_forms(w_qkv, w_out, *weights)

    def scan(a, count):
        for b in range(across - 1):
            value = code[a, b]
            picks[count] = ((a * WIN + HALF) * 256 + b * WIN + HALF) * 2 + value
            count = count + (value >= 0).astype(jnp.int32)
        upto[a] = count
        return count

    total = lax.fori_loop(0, chunks - 1, scan, jnp.int32(0))

    @pl.loop(0, chunks)
    def _(c):
        rows = pl.ds(c * WIN, WIN)
        result[:, rows] = jnp.zeros((2, WIN) + result.shape[2:], F32)

    marks[0] = 0
    marks[1] = 0

    def convert(until):
        @pl.loop(marks[0], until)
        def _(c):
            load(c, feat_hbm, feat_in, 0).wait()
            load(c, grad_hbm, grad_in, 1).wait()
            rows = pl.ds(c * WIN, WIN)
            feat[:, rows] = feat_in[:, rows].astype(F32)
            grad[:, rows] = grad_in[:, rows].astype(F32)

        marks[0] = jnp.maximum(marks[0], until)

    def before(n):
        row = picks[jnp.minimum(n, total - 1)] // 512
        convert((row + WIN - 1) // WIN + 1)

    def after(count):
        def put(s, stored):
            full = (s == stored) & (upto[s] <= jnp.minimum(count, total - 1))

            @pl.when(full)
            def _():
                store(s).start()

            return stored + full.astype(jnp.int32)

        marks[1] = lax.fori_loop(marks[1], chunks - 1, put, marks[1])

    run_windows(total, picks, feat, grad, result, weights, stash, before, after)
    convert(chunks)

    @pl.loop(marks[1], chunks - 1)
    def _(s):
        store(s).start()

    @pl.loop(0, chunks - 1)
    def _(s):
        store(s).wait()


def inner_windows(code, features, grad_out, w_qkv, w_out):
    shape = features.shape
    chunks = shape[1] // WIN
    hbm = pl.BlockSpec(memory_space=pl.ANY)
    vmem = pl.BlockSpec(memory_space=pltpu.VMEM)
    smem = pl.BlockSpec(memory_space=pltpu.SMEM)
    return pl.pallas_call(
        inner_kernel,
        out_shape=jax.ShapeDtypeStruct(shape, F32),
        in_specs=[smem, hbm, hbm, vmem, vmem],
        out_specs=hbm,
        scratch_shapes=[
            pltpu.VMEM(shape, BF16),
            pltpu.VMEM(shape, BF16),
            pltpu.VMEM(shape, F32),
            pltpu.VMEM(shape, F32),
            pltpu.VMEM(shape, F32),
            pltpu.SMEM((chunks * (shape[2] // WIN) + 1,), jnp.int32),
            pltpu.SMEM((chunks,), jnp.int32),
            pltpu.SMEM((2,), jnp.int32),
            pltpu.SemaphoreType.DMA((chunks, 2)),
            pltpu.SemaphoreType.DMA((chunks - 1,)),
            *WEIGHTS,
            *STASH,
        ],
        compiler_params=pltpu.CompilerParams(vmem_limit_bytes=48 * 2**20),
        cost_estimate=pl.CostEstimate(flops=105 * 235 * 10**6, bytes_accessed=16 * 2**20, transcendentals=105 * 65536),
        name="inner_windows",
    )(code, features, grad_out, w_qkv, w_out)


def edge_kernel(
    code, feat_hbm, grad_hbm, above, below, left, right, w_qkv, w_out, before, out_hbm,
    rows_in, cols_in, feat, grad, result, sides, picks, far_vector, far, in_sem, side_sem, far_sem, out_sem,
    *held,
):
    weights, stash = held[:3], held[3:]
    rows, cols = feat_hbm.shape[1], feat_hbm.shape[2]
    down, wide = rows // WIN + 1, cols // WIN + 1
    inner = rows - 2 * HALF
    copies = []
    for n, hbm in enumerate((feat_hbm, grad_hbm)):
        for m, at in enumerate((0, rows - HALF)):
            copies.append(pltpu.make_async_copy(hbm.at[:, pl.ds(at, HALF)], rows_in.at[n, m], in_sem.at[n, m]))
        for m, at in enumerate((0, cols - 16)):
            copies.append(
                pltpu.make_async_copy(
                    hbm.at[:, pl.ds(HALF, inner), pl.ds(at, 16)], cols_in.at[n, m], in_sem.at[n, 2 + m]
                )
            )
    for copy in copies:
        copy.start()
    side_at = (0, cols - WIN)
    side_in = [
        pltpu.make_async_copy(
            before.at[:, pl.ds(HALF, inner), pl.ds(at, WIN)], sides.at[m], side_sem.at[m]
        )
        for m, at in enumerate(side_at)
    ]
    for copy in side_in:
        copy.start()

    far_vector[: 2 * WIN] = above[0, 0, 0, cols + 2 * WIN :].astype(F32).astype(jnp.int32)
    far_vector[2 * WIN :] = left[0, 0, rows // 2].astype(F32).astype(jnp.int32)
    far_copy = pltpu.make_async_copy(far_vector, far, far_sem)
    far_copy.start()
    weight_forms(w_qkv, w_out, *weights)
    far_copy.wait()

    def pick(a, b, value, count):
        picks[count] = (a * WIN * 256 + b * WIN + HALF) * 2 + value
        return count + (value >= 0).astype(jnp.int32)

    last_row, last_col = down - 2, wide - 2
    total = pick(0, 0, far[WIN + last_row, last_col], jnp.int32(0))
    for b in range(1, wide):
        total = pick(0, b, far[last_row, b - 1], total)

    def scan(a, count):
        count = pick(a, 0, far[2 * WIN + a - 1, last_col], count)
        return pick(a, wide - 1, code[a - 1, last_col], count)

    total = lax.fori_loop(1, down - 1, scan, total)
    total = pick(down - 1, 0, far[2 * WIN + last_row, last_col], total)
    for b in range(1, wide):
        total = pick(down - 1, b, code[last_row, b - 1], total)

    for at in (0, rows):
        result[:, at : at + WIN] = jnp.zeros((2, WIN) + result.shape[2:], F32)
    for at in (0, cols):
        result[:, WIN:rows, at : at + 2 * WIN] = jnp.zeros((2, rows - WIN, 2 * WIN, CH), F32)

    for n, frame in enumerate((feat, grad)):
        frame[:, :HALF] = above[n, :, :, : cols + 2 * WIN].astype(F32)
        frame[:, rows + HALF :] = below[n, :, :, : cols + 2 * WIN].astype(F32)
        for side, at in ((left, 0), (right, cols + WIN)):
            value = side[n, :, : rows // 2].astype(F32).reshape(2, rows, WIN, CH)
            frame[:, HALF : rows + HALF, at : at + WIN] = value
    for copy in copies:
        copy.wait()
    for n, frame in enumerate((feat, grad)):
        frame[:, HALF : 2 * HALF, WIN : WIN + cols] = rows_in[n, 0].astype(F32)
        frame[:, rows : rows + HALF, WIN : WIN + cols] = rows_in[n, 1].astype(F32)
        frame[:, 2 * HALF : rows, WIN : WIN + 16] = cols_in[n, 0].astype(F32)
        frame[:, 2 * HALF : rows, cols - WIN : cols + WIN] = cols_in[n, 1].astype(F32)

    run_windows(
        total, picks, feat, grad, result, weights, stash,
        lambda n: None, lambda n: None,
    )

    back = [
        pltpu.make_async_copy(
            result.at[:, pl.ds(HALF, HALF), pl.ds(WIN, cols)], out_hbm.at[:, pl.ds(0, HALF)], out_sem.at[0]
        ),
        pltpu.make_async_copy(
            result.at[:, pl.ds(rows, HALF), pl.ds(WIN, cols)], out_hbm.at[:, pl.ds(rows - HALF, HALF)], out_sem.at[1]
        ),
    ]
    for m, at in enumerate(side_at):
        side_in[m].wait()
        first = 0 if m == 0 else HALF
        sides[m, :, :, first : first + HALF] = result[:, WIN:rows, WIN + at + first : WIN + at + first + HALF]
        back.append(
            pltpu.make_async_copy(
                sides.at[m], out_hbm.at[:, pl.ds(HALF, inner), pl.ds(at, WIN)], out_sem.at[2 + m]
            )
        )
    for copy in back:
        copy.start()
    for copy in back:
        copy.wait()


def edge_windows(code, features, grad_out, halos, w_qkv, w_out, before):
    shape = features.shape
    rows, cols = shape[1], shape[2]
    frame = (2, rows + 2 * HALF, cols + 2 * WIN, CH)
    hbm = pl.BlockSpec(memory_space=pl.ANY)
    vmem = pl.BlockSpec(memory_space=pltpu.VMEM)
    smem = pl.BlockSpec(memory_space=pltpu.SMEM)
    operands = (code, features, grad_out, *halos, w_qkv, w_out, before)
    return pl.pallas_call(
        edge_kernel,
        out_shape=jax.ShapeDtypeStruct(shape, F32),
        in_specs=[smem] + [hbm] * 2 + [vmem] * 6 + [hbm],
        out_specs=hbm,
        scratch_shapes=[
            pltpu.VMEM((2, 2, 2, HALF, cols, CH), BF16),
            pltpu.VMEM((2, 2, 2, rows - 2 * HALF, 16, CH), BF16),
            pltpu.VMEM(frame, F32),
            pltpu.VMEM(frame, F32),
            pltpu.VMEM(frame, F32),
            pltpu.VMEM((2, 2, rows - 2 * HALF, WIN, CH), F32),
            pltpu.SMEM(((rows // WIN + 1) * (cols // WIN + 1) + 1,), jnp.int32),
            pltpu.VMEM((4 * WIN, CH), jnp.int32),
            pltpu.SMEM((4 * WIN, CH), jnp.int32),
            pltpu.SemaphoreType.DMA((2, 4)),
            pltpu.SemaphoreType.DMA((2,)),
            pltpu.SemaphoreType.DMA,
            pltpu.SemaphoreType.DMA((4,)),
            *WEIGHTS,
            *STASH,
        ],
        input_output_aliases={len(operands) - 1: 0},
        compiler_params=pltpu.CompilerParams(vmem_limit_bytes=56 * 2**20),
        cost_estimate=pl.CostEstimate(flops=48 * 235 * 10**6, bytes_accessed=8 * 2**20, transcendentals=48 * 65536),
        name="edge_windows",
    )(*operands)


def column_kernel(route, feat_hbm, grad_hbm, cross, west, east, code, cols_in, page, in_sem):
    rows, cols = feat_hbm.shape[1], feat_hbm.shape[2]
    copies = [
        pltpu.make_async_copy(
            hbm.at[:, :, pl.ds(at, 2 * WIN)], cols_in.at[n, m], in_sem.at[n, m]
        )
        for n, hbm in enumerate((feat_hbm, grad_hbm))
        for m, at in enumerate((0, cols - 2 * WIN))
    ]
    for copy in copies:
        copy.start()
    shape = cross.shape
    ids = lax.broadcasted_iota(jnp.int32, shape, 0) * shape[1] + lax.broadcasted_iota(jnp.int32, shape, 1)
    live = jnp.zeros(shape, jnp.int32)
    for d in range(route.shape[2]):
        for s in range(route.shape[3]):
            live = jnp.where(ids == route[0, 0, d, s], 1, live)
    value = jnp.where(live > 0, jnp.where(cross[...] > 0, 1, 0), -1)
    code[...] = value
    page[...] = jnp.zeros_like(page)
    page[: shape[0], : shape[1]] = value.astype(F32)
    for out in (west, east):
        for n in range(2):
            for v in range(2):
                out[n, v, rows // 2] = page[...].astype(BF16)
    for copy in copies:
        copy.wait()
    for n in range(2):
        for m, out in enumerate((west, east)):
            edge = cols_in[n, m].astype(F32)[:, :, WIN * m : WIN * m + WIN]
            out[n, :, : rows // 2] = edge.reshape(2, rows // 2, 2 * WIN, CH).astype(BF16)


def pack_columns(features, grad_out, cross_live, route):
    _, rows, cols, _ = features.shape
    hbm = pl.BlockSpec(memory_space=pl.ANY)
    vmem = pl.BlockSpec(memory_space=pltpu.VMEM)
    smem = pl.BlockSpec(memory_space=pltpu.SMEM)
    edge = jax.ShapeDtypeStruct((2, 2, rows // 2 + 1, 2 * WIN, CH), BF16)
    return pl.pallas_call(
        column_kernel,
        out_shape=(edge, edge, jax.ShapeDtypeStruct(cross_live.shape, jnp.int32)),
        in_specs=[smem, hbm, hbm, vmem],
        out_specs=(vmem, vmem, vmem),
        scratch_shapes=[
            pltpu.VMEM((2, 2, 2, rows, 2 * WIN, CH), BF16),
            pltpu.VMEM((2 * WIN, CH), F32),
            pltpu.SemaphoreType.DMA((2, 2)),
        ],
        compiler_params=pltpu.CompilerParams(vmem_limit_bytes=60 * 2**20),
        name="pack_columns",
    )(route, features, grad_out, cross_live)


def row_kernel(feat_hbm, grad_hbm, left, right, code, north, south, code_out, rows_in, page, in_sem):
    rows = feat_hbm.shape[1]
    copies = [
        pltpu.make_async_copy(hbm.at[:, pl.ds(at, HALF)], rows_in.at[n, m], in_sem.at[n, m])
        for n, hbm in enumerate((feat_hbm, grad_hbm))
        for m, at in enumerate((0, rows - HALF))
    ]
    for copy in copies:
        copy.start()
    code_out[...] = code[...]
    height, width = code.shape
    page[...] = jnp.zeros_like(page)
    page[:height, :width] = code[...].astype(F32)
    page[WIN:] = left[0, 0, rows // 2].astype(F32)[:WIN]
    for copy in copies:
        copy.wait()
    tail = jnp.broadcast_to(page[...], (2, HALF, 2 * WIN, CH))
    for n in range(2):
        for m, out in enumerate((north, south)):
            part = slice(0, HALF // 2) if m == 0 else slice(rows // 2 - HALF // 2, rows // 2)
            sides = [side[n, :, part].astype(F32).reshape(2, HALF, WIN, CH) for side in (left, right)]
            whole = cat([sides[0], rows_in[n, m].astype(F32), sides[1], tail], 2)
            out[n] = whole.astype(BF16)


def pack_rows(features, grad_out, left, right, code):
    _, rows, cols, _ = features.shape
    hbm = pl.BlockSpec(memory_space=pl.ANY)
    vmem = pl.BlockSpec(memory_space=pltpu.VMEM)
    edge = jax.ShapeDtypeStruct((2, 2, HALF, cols + 4 * WIN, CH), BF16)
    return pl.pallas_call(
        row_kernel,
        out_shape=(edge, edge, jax.ShapeDtypeStruct(code.shape, jnp.int32)),
        in_specs=[hbm, hbm, vmem, vmem, vmem],
        out_specs=(vmem, vmem, vmem),
        scratch_shapes=[
            pltpu.VMEM((2, 2, 2, HALF, cols, CH), BF16),
            pltpu.VMEM((2 * WIN, CH), F32),
            pltpu.SemaphoreType.DMA((2, 2)),
        ],
        compiler_params=pltpu.CompilerParams(vmem_limit_bytes=60 * 2**20),
        name="pack_rows",
    )(features, grad_out, left, right, code)


def moved(value, axis, steps):
    count = lax.axis_size(axis)
    return lax.ppermute(value, axis, [(n, (n + steps) % count) for n in range(count)])


def on_device(features, grad_out, w_qkv, w_out, cross_live, route):
    west, east, code = pack_columns(features, grad_out, cross_live, route.transpose(0, 1, 3, 2))
    left, right = moved(east, "col", 1), moved(west, "col", -1)
    north, south, code = pack_rows(features, grad_out, left, right, code)
    above, below = moved(south, "row", 1), moved(north, "row", -1)
    inner = inner_windows(code, features, grad_out, w_qkv, w_out)
    halos = (above, below, left, right)
    return edge_windows(code, features, grad_out, halos, w_qkv, w_out, inner)


def solution(mesh):
    return jax.shard_map(
        on_device,
        mesh=mesh,
        in_specs=(
            P(None, "row", "col", None),
            P(None, "row", "col", None),
            P(),
            P(),
            P("row", "col"),
            P("row", "col", None, None),
        ),
        out_specs=P(None, "row", "col", None),
        check_vma=False,
    )
```

```python
import functools
import math

import jax
import jax.numpy as jnp
from jax import lax
from jax.experimental import pallas as pl
from jax.experimental.pallas import tpu as pltpu
from jax.sharding import PartitionSpec as P

F32 = jnp.float32
BF16 = jnp.bfloat16
HEADS = 4
WIN = 8
HALF = 4
CH = 128
HEAD = CH // HEADS
TOK = WIN * WIN
GROUP = 4
NEG = -1e30
LOG2E = math.log2(math.e)
SCALE = 1.0 / math.sqrt(HEAD)


def split(value):
    high = value.astype(BF16)
    return high, (value - high.astype(F32)).astype(BF16)


def mm(a, b):
    return lax.dot_general(a, b, (((1,), (0,)), ((), ())), preferred_element_type=F32)


def mm_nt(a, b):
    return lax.dot_general(a, b, (((1,), (1,)), ((), ())), preferred_element_type=F32)


def cat(parts, axis):
    return jnp.concatenate(parts, axis=axis)


def head_pair_rows(high, low, pair):
    zero = jnp.zeros((HEAD, 2 * TOK), BF16)
    zeros = jnp.zeros((2 * HEAD, 4 * TOK), BF16)
    first, second = (slice(HEAD * h, HEAD * h + HEAD) for h in (2 * pair, 2 * pair + 1))
    top = [cat([high[first], zero], 1), cat([zero, high[second]], 1)]
    fix = [cat([low[first], zero], 1), cat([zero, low[second]], 1)]
    tail = fix + [zeros] if pair == 0 else [zeros] + fix
    return cat(top + top + tail, 0)


def pair_product(tokens, columns, pair):
    lanes = slice(2 * HEAD * pair, 2 * HEAD * pair + 2 * HEAD)
    left = cat([tokens[0][:, lanes], tokens[1][:, lanes], tokens[0]], 1)
    return mm(left, head_pair_rows(columns[0], columns[1], pair))


def across_parts(across):
    return [split(across[CH * n : CH * n + CH]) for n in range(3)]


def project(window_feats, window_grads, weights):
    w_across, w_along = weights[0][...], weights[1][...]
    feats = cat(window_feats, 0)
    across = mm(w_across, cat([cat([f.T for f in part], 1) for part in (window_feats, window_grads)], 0))
    along = mm(cat([feats, feats], 1), w_along)
    out = []
    for n in range(len(window_feats)):
        part = slice(2 * TOK * n, 2 * TOK * n + 2 * TOK)
        out.append(
            across_parts(across[:, part]) + [split(along[part, :CH]), split(along[part, CH:])]
        )
    return out


def products(parts, pair):
    query, _, cotangent, keys, values = parts
    return pair_product(keys, query, pair), pair_product(values, cotangent, pair)


def soften(flag, scores, d_prob):
    lane = lax.broadcasted_iota(jnp.int32, (1, 4 * TOK), 1) % (2 * TOK)
    drop = jnp.where(flag > 0, 0.0, NEG).astype(F32)
    bias0 = jnp.where(lane < TOK, 0.0, drop)
    bias1 = jnp.where(lane < TOK, drop, 0.0)
    peak = jnp.maximum(
        jnp.max(scores[:TOK], axis=0, keepdims=True) + bias0,
        jnp.max(scores[TOK:], axis=0, keepdims=True) + bias1,
    )
    weight = cat(
        [jnp.exp2(scores[:TOK] - (peak - bias0)), jnp.exp2(scores[TOK:] - (peak - bias1))], 0
    )
    prob = weight * (1.0 / jnp.sum(weight, axis=0, keepdims=True))
    term = prob * d_prob
    d_score = term - prob * jnp.sum(term, axis=0, keepdims=True)
    prob, d_score = split(prob), split(d_score)
    turned = [
        cat([cat([half[:, : 2 * TOK].T, half[:, 2 * TOK :].T], 1) for half in value], 0)
        for value in (prob, d_score)
    ]
    return cat(d_score, 0), turned[0], turned[1]


def gather(sides, soft):
    by_key, prob, by_query = soft
    out = []
    for side, right in ((sides[1], by_key), (sides[0], by_query), (sides[2], prob)):
        left = cat([side[0][:HEAD], side[1][:HEAD], side[0][HEAD:], side[1][HEAD:]], 0)
        both = mm(cat([left, left], 1), right)
        first, second = both[: 2 * HEAD, : 2 * TOK], both[2 * HEAD :, 2 * TOK :]
        out.append(cat([first[:HEAD] + first[HEAD:], second[:HEAD] + second[HEAD:]], 0))
    return out


def pair_sides(parts, pair):
    rows = slice(2 * HEAD * pair, 2 * HEAD * pair + 2 * HEAD)
    return [(part[0][rows], part[1][rows]) for part in parts[:3]]


def finish(grads, w_back):
    whole = cat([cat([g[p][n] for n in range(3) for p in range(2)], 0) for g in grads], 1)
    out = mm(w_back[...], cat(split(whole), 0))
    return [out[:, 2 * TOK * n : 2 * TOK * n + 2 * TOK].T for n in range(len(grads))]


def weight_forms(w_qkv, w_out, w_across, w_along, w_back):
    zeros = jnp.zeros((CH, CH), BF16)
    for n in range(2):
        rows = slice(CH * n, CH * n + CH)
        w_across[rows, :CH] = w_qkv[:, rows].T
        w_across[rows, CH:] = zeros
    w_across[2 * CH :, :CH] = zeros
    w_across[2 * CH :, CH:] = w_out[...]
    for n, scale in enumerate((LOG2E * SCALE, SCALE)):
        cols = slice(CH * n, CH * n + CH)
        halves = split(w_qkv[:, CH + CH * n : 2 * CH + CH * n].astype(F32) * scale)
        for half in range(2):
            w_along[CH * half : CH * half + CH, cols] = halves[half]
    for half in range(2):
        w_back[:, 3 * CH * half : 3 * CH * half + 3 * CH] = w_qkv[...]


WEIGHTS = [
    pltpu.VMEM((3 * CH, 2 * CH), BF16),
    pltpu.VMEM((2 * CH, 2 * CH), BF16),
    pltpu.VMEM((CH, 6 * CH), BF16),
]


STASH = [
    pltpu.VMEM((2, 10, CH, 2 * TOK), BF16),
    pltpu.VMEM((2, 2 * TOK, 4 * TOK), F32),
    pltpu.VMEM((3, 4 * TOK, 4 * TOK), BF16),
    pltpu.VMEM((6, 2 * HEAD, 2 * TOK), BF16),
    pltpu.VMEM((3, 3, 2 * HEAD, 2 * TOK), F32),
]


def run_windows(total, picks, feat, grad, result, weights, stash, before, after):
    ahead, scored, softened, sided, kept = stash
    groups = (total + GROUP - 1) // GROUP

    def place(n):
        pick = picks[jnp.clip(n, 0, total - 1)]
        return pick // 512, (pick // 2) % 256, pick % 2

    def window(ref, n):
        row, col, _ = place(n)
        value = ref[:, pl.ds(row, WIN), pl.ds(col, WIN), :]
        return value.reshape(2 * TOK, CH).astype(BF16)

    def projected(n):
        return project(
            [window(feat, n), window(feat, n + 1)], [window(grad, n), window(grad, n + 1)], weights
        )

    def put(n, value):
        row, col, _ = place(n)
        result[:, pl.ds(row, WIN), pl.ds(col, WIN), :] = value.reshape(2, WIN, WIN, CH)

    def stash_ahead(parts):
        for w in range(2):
            for n in range(5):
                for half in range(2):
                    ahead[w, 2 * n + half] = parts[w][n][half]
        scored[0], scored[1] = products(parts[0], 0)

    def close(first):
        soft = [softened[n] for n in range(3)]
        last = gather([(sided[2 * n], sided[2 * n + 1]) for n in range(3)], soft)
        held = [[kept[u, n] for n in range(3)] for u in range(3)]
        for n, value in enumerate(finish([held[:2], [held[2], last]], weights[2])):
            put(first - 2 + n, value)

    @pl.when(total > 0)
    def _():
        before(1)
        stash_ahead(projected(0))

    @pl.loop(0, groups)
    def _(i):
        first = i * GROUP
        before(first + GROUP + 1)
        parts = [
            [(ahead[w, 2 * n], ahead[w, 2 * n + 1]) for n in range(5)] for w in range(2)
        ] + [None, None]
        flags = [place(first + n)[2] for n in range(GROUP)]
        ready = {0: (scored[0], scored[1])}
        soft, done = {}, {}
        for u in range(2 * GROUP):
            if u < 2 * GROUP - 1:
                ready[u + 1] = products(parts[(u + 1) // 2], (u + 1) % 2)
            else:
                stash_ahead(following)
            soft[u] = soften(flags[u // 2], *ready.pop(u))
            if u == 0:
                close(first)
                parts[2:] = projected(first + 2)
            else:
                v = u - 1
                done[v] = gather(pair_sides(parts[v // 2], v % 2), soft.pop(v))
            if u == 4:
                outs = finish([[done[0], done[1]], [done[2], done[3]]], weights[2])
                for n, value in enumerate(outs):
                    put(first + n, value)
            if u == 5:
                following = projected(first + GROUP)
        end = soft.pop(2 * GROUP - 1)
        for n in range(3):
            softened[n] = end[n]
        for n, side in enumerate(pair_sides(parts[-1], 1)):
            sided[2 * n], sided[2 * n + 1] = side
        for n, u in enumerate((4, 5, 6)):
            for m in range(3):
                kept[n, m] = done[u][m]
        after(first + 2)

    @pl.when(total > 0)
    def _():
        close(groups * GROUP)


def inner_kernel(
    code, feat_hbm, grad_hbm, w_qkv, w_out, out_hbm,
    feat_in, grad_in, feat, grad, result, picks, upto, marks, in_sem, out_sem, *held,
):
    weights, stash = held[:3], held[3:]
    chunks = feat.shape[1] // WIN
    across = feat.shape[2] // WIN

    def load(c, hbm, buf, which):
        rows = pl.ds(c * WIN, WIN)
        return pltpu.make_async_copy(hbm.at[:, rows], buf.at[:, rows], in_sem.at[c, which])

    def store(s):
        rows = pl.ds(s * WIN + HALF, WIN)
        return pltpu.make_async_copy(result.at[:, rows], out_hbm.at[:, rows], out_sem.at[s])

    @pl.loop(0, chunks)
    def _(c):
        load(c, feat_hbm, feat_in, 0).start()
        load(c, grad_hbm, grad_in, 1).start()

    weight_forms(w_qkv, w_out, *weights)

    def scan(a, count):
        for b in range(across - 1):
            value = code[a, b]
            picks[count] = ((a * WIN + HALF) * 256 + b * WIN + HALF) * 2 + value
            count = count + (value >= 0).astype(jnp.int32)
        upto[a] = count
        return count

    total = lax.fori_loop(0, chunks - 1, scan, jnp.int32(0))

    @pl.loop(0, chunks)
    def _(c):
        rows = pl.ds(c * WIN, WIN)
        result[:, rows] = jnp.zeros((2, WIN) + result.shape[2:], F32)

    marks[0] = 0
    marks[1] = 0

    def convert(until):
        @pl.loop(marks[0], until)
        def _(c):
            load(c, feat_hbm, feat_in, 0).wait()
            load(c, grad_hbm, grad_in, 1).wait()
            rows = pl.ds(c * WIN, WIN)
            feat[:, rows] = feat_in[:, rows].astype(F32)
            grad[:, rows] = grad_in[:, rows].astype(F32)

        marks[0] = jnp.maximum(marks[0], until)

    def before(n):
        row = picks[jnp.minimum(n, total - 1)] // 512
        convert((row + WIN - 1) // WIN + 1)

    def after(count):
        s = marks[1]
        full = (s < chunks - 1) & (upto[jnp.minimum(s, chunks - 2)] <= jnp.minimum(count, total - 1))

        @pl.when(full)
        def _():
            store(s).start()
            marks[1] = s + 1

    run_windows(total, picks, feat, grad, result, weights, stash, before, after)
    convert(chunks)

    @pl.loop(marks[1], chunks - 1)
    def _(s):
        store(s).start()

    @pl.loop(0, chunks - 1)
    def _(s):
        store(s).wait()


def inner_windows(code, features, grad_out, w_qkv, w_out):
    shape = features.shape
    chunks = shape[1] // WIN
    hbm = pl.BlockSpec(memory_space=pl.ANY)
    vmem = pl.BlockSpec(memory_space=pltpu.VMEM)
    smem = pl.BlockSpec(memory_space=pltpu.SMEM)
    return pl.pallas_call(
        inner_kernel,
        out_shape=jax.ShapeDtypeStruct(shape, F32),
        in_specs=[smem, hbm, hbm, vmem, vmem],
        out_specs=hbm,
        scratch_shapes=[
            pltpu.VMEM(shape, BF16),
            pltpu.VMEM(shape, BF16),
            pltpu.VMEM(shape, F32),
            pltpu.VMEM(shape, F32),
            pltpu.VMEM(shape, F32),
            pltpu.SMEM((chunks * (shape[2] // WIN) + 1,), jnp.int32),
            pltpu.SMEM((chunks,), jnp.int32),
            pltpu.SMEM((2,), jnp.int32),
            pltpu.SemaphoreType.DMA((chunks, 2)),
            pltpu.SemaphoreType.DMA((chunks - 1,)),
            *WEIGHTS,
            *STASH,
        ],
        compiler_params=pltpu.CompilerParams(vmem_limit_bytes=60 * 2**20),
        cost_estimate=pl.CostEstimate(flops=105 * 235 * 10**6, bytes_accessed=16 * 2**20, transcendentals=105 * 65536),
        name="inner_windows",
    )(code, features, grad_out, w_qkv, w_out)


def edge_kernel(
    code, feat_hbm, grad_hbm, above, below, left, right, w_qkv, w_out, before, out_hbm,
    rows_in, cols_in, feat, grad, result, sides, picks, far_vector, far, in_sem, side_sem, far_sem, out_sem,
    *held,
):
    weights, stash = held[:3], held[3:]
    rows, cols = feat_hbm.shape[1], feat_hbm.shape[2]
    down, wide = rows // WIN + 1, cols // WIN + 1
    inner = rows - 2 * HALF
    copies = []
    for n, hbm in enumerate((feat_hbm, grad_hbm)):
        for m, at in enumerate((0, rows - HALF)):
            copies.append(pltpu.make_async_copy(hbm.at[:, pl.ds(at, HALF)], rows_in.at[n, m], in_sem.at[n, m]))
        for m, at in enumerate((0, cols - 16)):
            copies.append(
                pltpu.make_async_copy(
                    hbm.at[:, pl.ds(HALF, inner), pl.ds(at, 16)], cols_in.at[n, m], in_sem.at[n, 2 + m]
                )
            )
    for copy in copies:
        copy.start()
    side_at = (0, cols - WIN)
    side_in = [
        pltpu.make_async_copy(
            before.at[:, pl.ds(HALF, inner), pl.ds(at, WIN)], sides.at[m], side_sem.at[m]
        )
        for m, at in enumerate(side_at)
    ]
    for copy in side_in:
        copy.start()

    far_vector[: 2 * WIN] = above[0, 0, 0, cols + 2 * WIN :].astype(F32).astype(jnp.int32)
    far_vector[2 * WIN :] = left[0, 0, rows // 4].astype(F32).astype(jnp.int32)
    far_copy = pltpu.make_async_copy(far_vector, far, far_sem)
    far_copy.start()
    weight_forms(w_qkv, w_out, *weights)
    far_copy.wait()

    def pick(a, b, value, count):
        picks[count] = (a * WIN * 256 + b * WIN + HALF) * 2 + value
        return count + (value >= 0).astype(jnp.int32)

    last_row, last_col = down - 2, wide - 2
    total = pick(0, 0, far[WIN + last_row, last_col], jnp.int32(0))
    for b in range(1, wide):
        total = pick(0, b, far[last_row, b - 1], total)

    def scan(a, count):
        count = pick(a, 0, far[2 * WIN + a - 1, last_col], count)
        return pick(a, wide - 1, code[a - 1, last_col], count)

    total = lax.fori_loop(1, down - 1, scan, total)
    total = pick(down - 1, 0, far[2 * WIN + last_row, last_col], total)
    for b in range(1, wide):
        total = pick(down - 1, b, code[last_row, b - 1], total)

    for at in (0, rows):
        result[:, at : at + WIN] = jnp.zeros((2, WIN) + result.shape[2:], F32)
    for at in (0, cols):
        result[:, WIN:rows, at : at + 2 * WIN] = jnp.zeros((2, rows - WIN, 2 * WIN, CH), F32)

    for n, frame in enumerate((feat, grad)):
        frame[:, :HALF] = above[n, :, :, : cols + 2 * WIN].astype(F32)
        frame[:, rows + HALF :] = below[n, :, :, : cols + 2 * WIN].astype(F32)
        for side, at in ((left, HALF), (right, cols + WIN)):
            value = side[n, :, : rows // 4].astype(F32).reshape(2, rows // 2, WIN, CH)
            for half in range(2):
                first = HALF + half * (rows // 2)
                part = value[:, :, HALF * half : HALF * half + HALF]
                frame[:, first : first + rows // 2, at : at + HALF] = part
    for copy in copies:
        copy.wait()
    for n, frame in enumerate((feat, grad)):
        frame[:, HALF : 2 * HALF, WIN : WIN + cols] = rows_in[n, 0].astype(F32)
        frame[:, rows : rows + HALF, WIN : WIN + cols] = rows_in[n, 1].astype(F32)
        frame[:, 2 * HALF : rows, WIN : WIN + 16] = cols_in[n, 0].astype(F32)
        frame[:, 2 * HALF : rows, cols - WIN : cols + WIN] = cols_in[n, 1].astype(F32)

    run_windows(
        total, picks, feat, grad, result, weights, stash,
        lambda n: None, lambda n: None,
    )

    back = [
        pltpu.make_async_copy(
            result.at[:, pl.ds(HALF, HALF), pl.ds(WIN, cols)], out_hbm.at[:, pl.ds(0, HALF)], out_sem.at[0]
        ),
        pltpu.make_async_copy(
            result.at[:, pl.ds(rows, HALF), pl.ds(WIN, cols)], out_hbm.at[:, pl.ds(rows - HALF, HALF)], out_sem.at[1]
        ),
    ]
    for m, at in enumerate(side_at):
        side_in[m].wait()
        first = 0 if m == 0 else HALF
        sides[m, :, :, first : first + HALF] = result[:, WIN:rows, WIN + at + first : WIN + at + first + HALF]
        back.append(
            pltpu.make_async_copy(
                sides.at[m], out_hbm.at[:, pl.ds(HALF, inner), pl.ds(at, WIN)], out_sem.at[2 + m]
            )
        )
    for copy in back:
        copy.start()
    for copy in back:
        copy.wait()


def edge_windows(code, features, grad_out, halos, w_qkv, w_out, before):
    shape = features.shape
    rows, cols = shape[1], shape[2]
    frame = (2, rows + 2 * HALF, cols + 2 * WIN, CH)
    hbm = pl.BlockSpec(memory_space=pl.ANY)
    vmem = pl.BlockSpec(memory_space=pltpu.VMEM)
    smem = pl.BlockSpec(memory_space=pltpu.SMEM)
    operands = (code, features, grad_out, *halos, w_qkv, w_out, before)
    return pl.pallas_call(
        edge_kernel,
        out_shape=jax.ShapeDtypeStruct(shape, F32),
        in_specs=[smem] + [hbm] * 2 + [vmem] * 6 + [hbm],
        out_specs=hbm,
        scratch_shapes=[
            pltpu.VMEM((2, 2, 2, HALF, cols, CH), BF16),
            pltpu.VMEM((2, 2, 2, rows - 2 * HALF, 16, CH), BF16),
            pltpu.VMEM(frame, F32),
            pltpu.VMEM(frame, F32),
            pltpu.VMEM(frame, F32),
            pltpu.VMEM((2, 2, rows - 2 * HALF, WIN, CH), F32),
            pltpu.SMEM(((rows // WIN + 1) * (cols // WIN + 1) + 1,), jnp.int32),
            pltpu.VMEM((4 * WIN, CH), jnp.int32),
            pltpu.SMEM((4 * WIN, CH), jnp.int32),
            pltpu.SemaphoreType.DMA((2, 4)),
            pltpu.SemaphoreType.DMA((2,)),
            pltpu.SemaphoreType.DMA,
            pltpu.SemaphoreType.DMA((4,)),
            *WEIGHTS,
            *STASH,
        ],
        input_output_aliases={len(operands) - 1: 0},
        compiler_params=pltpu.CompilerParams(vmem_limit_bytes=56 * 2**20),
        cost_estimate=pl.CostEstimate(flops=48 * 235 * 10**6, bytes_accessed=8 * 2**20, transcendentals=48 * 65536),
        name="edge_windows",
    )(*operands)


def column_kernel(route, feat_hbm, grad_hbm, cross, west, east, code, cols_in, page, in_sem):
    rows, cols = feat_hbm.shape[1], feat_hbm.shape[2]
    copies = [
        pltpu.make_async_copy(
            hbm.at[:, :, pl.ds(at, 2 * WIN)], cols_in.at[n, m], in_sem.at[n, m]
        )
        for n, hbm in enumerate((feat_hbm, grad_hbm))
        for m, at in enumerate((0, cols - 2 * WIN))
    ]
    for copy in copies:
        copy.start()
    shape = cross.shape
    ids = lax.broadcasted_iota(jnp.int32, shape, 0) * shape[1] + lax.broadcasted_iota(jnp.int32, shape, 1)
    live = jnp.zeros(shape, jnp.int32)
    for d in range(route.shape[2]):
        for s in range(route.shape[3]):
            live = jnp.where(ids == route[0, 0, d, s], 1, live)
    value = jnp.where(live > 0, jnp.where(cross[...] > 0, 1, 0), -1)
    code[...] = value
    page[...] = jnp.zeros_like(page)
    page[: shape[0], : shape[1]] = value.astype(F32)
    for out in (west, east):
        for n in range(2):
            for v in range(2):
                out[n, v, rows // 4] = page[...].astype(BF16)
    for copy in copies:
        copy.wait()
    upper = lax.broadcasted_iota(jnp.int32, (1, 1, WIN, CH), 2) < HALF
    for n in range(2):
        for m, out in enumerate((west, east)):
            edge = cols_in[n, m].astype(F32)[:, :, WIN * m : WIN * m + WIN]
            first, second = edge[:, : rows // 2], edge[:, rows // 2 :]
            if m == 0:
                value = jnp.where(upper, first, pltpu.roll(second, HALF, 2))
            else:
                value = jnp.where(upper, pltpu.roll(first, HALF, 2), second)
            out[n, :, : rows // 4] = value.reshape(2, rows // 4, 2 * WIN, CH).astype(BF16)


def pack_columns(features, grad_out, cross_live, route):
    _, rows, cols, _ = features.shape
    hbm = pl.BlockSpec(memory_space=pl.ANY)
    vmem = pl.BlockSpec(memory_space=pltpu.VMEM)
    smem = pl.BlockSpec(memory_space=pltpu.SMEM)
    edge = jax.ShapeDtypeStruct((2, 2, rows // 4 + 1, 2 * WIN, CH), BF16)
    return pl.pallas_call(
        column_kernel,
        out_shape=(edge, edge, jax.ShapeDtypeStruct(cross_live.shape, jnp.int32)),
        in_specs=[smem, hbm, hbm, vmem],
        out_specs=(vmem, vmem, vmem),
        scratch_shapes=[
            pltpu.VMEM((2, 2, 2, rows, 2 * WIN, CH), BF16),
            pltpu.VMEM((2 * WIN, CH), F32),
            pltpu.SemaphoreType.DMA((2, 2)),
        ],
        compiler_params=pltpu.CompilerParams(vmem_limit_bytes=52 * 2**20),
        name="pack_columns",
    )(route, features, grad_out, cross_live)


def row_kernel(feat_hbm, grad_hbm, left, right, code, north, south, code_out, rows_in, page, in_sem):
    rows = feat_hbm.shape[1]
    copies = [
        pltpu.make_async_copy(hbm.at[:, pl.ds(at, HALF)], rows_in.at[n, m], in_sem.at[n, m])
        for n, hbm in enumerate((feat_hbm, grad_hbm))
        for m, at in enumerate((0, rows - HALF))
    ]
    for copy in copies:
        copy.start()
    code_out[...] = code[...]
    height, width = code.shape
    page[...] = jnp.zeros_like(page)
    page[:height, :width] = code[...].astype(F32)
    page[WIN:] = left[0, 0, rows // 4].astype(F32)[:WIN]
    for copy in copies:
        copy.wait()
    tail = jnp.broadcast_to(page[...], (2, HALF, 2 * WIN, CH))
    for n in range(2):
        for m, out in enumerate((north, south)):
            part = slice(0, HALF // 2) if m == 0 else slice(rows // 4 - HALF // 2, rows // 4)
            sides = [side[n, :, part].astype(F32).reshape(2, HALF, WIN, CH) for side in (left, right)]
            sides[m] = pltpu.roll(sides[m], HALF, 2)
            whole = cat([sides[0], rows_in[n, m].astype(F32), sides[1], tail], 2)
            out[n] = whole.astype(BF16)


def pack_rows(features, grad_out, left, right, code):
    _, rows, cols, _ = features.shape
    hbm = pl.BlockSpec(memory_space=pl.ANY)
    vmem = pl.BlockSpec(memory_space=pltpu.VMEM)
    edge = jax.ShapeDtypeStruct((2, 2, HALF, cols + 4 * WIN, CH), BF16)
    return pl.pallas_call(
        row_kernel,
        out_shape=(edge, edge, jax.ShapeDtypeStruct(code.shape, jnp.int32)),
        in_specs=[hbm, hbm, vmem, vmem, vmem],
        out_specs=(vmem, vmem, vmem),
        scratch_shapes=[
            pltpu.VMEM((2, 2, 2, HALF, cols, CH), BF16),
            pltpu.VMEM((2 * WIN, CH), F32),
            pltpu.SemaphoreType.DMA((2, 2)),
        ],
        compiler_params=pltpu.CompilerParams(vmem_limit_bytes=52 * 2**20),
        name="pack_rows",
    )(features, grad_out, left, right, code)


def moved(value, axis, steps):
    count = lax.axis_size(axis)
    return lax.ppermute(value, axis, [(n, (n + steps) % count) for n in range(count)])


def on_device(features, grad_out, w_qkv, w_out, cross_live, route):
    west, east, code = pack_columns(features, grad_out, cross_live, route.transpose(0, 1, 3, 2))
    left, right = moved(east, "col", 1), moved(west, "col", -1)
    north, south, code = pack_rows(features, grad_out, left, right, code)
    above, below = moved(south, "row", 1), moved(north, "row", -1)
    inner = inner_windows(code, features, grad_out, w_qkv, w_out)
    halos = (above, below, left, right)
    return edge_windows(code, features, grad_out, halos, w_qkv, w_out, inner)


def solution(mesh):
    return jax.shard_map(
        on_device,
        mesh=mesh,
        in_specs=(
            P(None, "row", "col", None),
            P(None, "row", "col", None),
            P(),
            P(),
            P("row", "col"),
            P("row", "col", None, None),
        ),
        out_specs=P(None, "row", "col", None),
        check_vma=False,
    )
```

```python
import functools
import math

import jax
import jax.numpy as jnp
from jax import lax
from jax.experimental import pallas as pl
from jax.experimental.pallas import tpu as pltpu
from jax.sharding import PartitionSpec as P

F32 = jnp.float32
BF16 = jnp.bfloat16
HEADS = 4
WIN = 8
HALF = 4
CH = 128
HEAD = CH // HEADS
TOK = WIN * WIN
GROUP = 4
NEG = -1e30
LOG2E = math.log2(math.e)
SCALE = 1.0 / math.sqrt(HEAD)


def split(value):
    high = value.astype(BF16)
    return high, (value - high.astype(F32)).astype(BF16)


def mm(a, b):
    return lax.dot_general(a, b, (((1,), (0,)), ((), ())), preferred_element_type=F32)


def mm_nt(a, b):
    return lax.dot_general(a, b, (((1,), (1,)), ((), ())), preferred_element_type=F32)


def cat(parts, axis):
    return jnp.concatenate(parts, axis=axis)


def head_pair_rows(high, low, pair):
    zero = jnp.zeros((HEAD, 2 * TOK), BF16)
    zeros = jnp.zeros((2 * HEAD, 4 * TOK), BF16)
    first, second = (slice(HEAD * h, HEAD * h + HEAD) for h in (2 * pair, 2 * pair + 1))
    top = [cat([high[first], zero], 1), cat([zero, high[second]], 1)]
    fix = [cat([low[first], zero], 1), cat([zero, low[second]], 1)]
    tail = fix + [zeros] if pair == 0 else [zeros] + fix
    return cat(top + top + tail, 0)


def pair_product(tokens, columns, pair):
    lanes = slice(2 * HEAD * pair, 2 * HEAD * pair + 2 * HEAD)
    left = cat([tokens[0][:, lanes], tokens[1][:, lanes], tokens[0]], 1)
    return mm(left, head_pair_rows(columns[0], columns[1], pair))


def across_parts(across):
    return [split(across[CH * n : CH * n + CH]) for n in range(3)]


def project(window_feats, window_grads, weights):
    w_across, w_along = weights[0][...], weights[1][...]
    feats = cat(window_feats, 0)
    across = mm(w_across, cat([cat([f.T for f in part], 1) for part in (window_feats, window_grads)], 0))
    along = mm(cat([feats, feats], 1), w_along)
    out = []
    for n in range(len(window_feats)):
        part = slice(2 * TOK * n, 2 * TOK * n + 2 * TOK)
        out.append(
            across_parts(across[:, part]) + [split(along[part, :CH]), split(along[part, CH:])]
        )
    return out


def products(parts, pair):
    query, _, cotangent, keys, values = parts
    return pair_product(keys, query, pair), pair_product(values, cotangent, pair)


def soften(flag, scores, d_prob):
    lane = lax.broadcasted_iota(jnp.int32, (1, 4 * TOK), 1) % (2 * TOK)
    drop = jnp.where(flag > 0, 0.0, NEG).astype(F32)
    bias0 = jnp.where(lane < TOK, 0.0, drop)
    bias1 = jnp.where(lane < TOK, drop, 0.0)
    peak = jnp.maximum(
        jnp.max(scores[:TOK], axis=0, keepdims=True) + bias0,
        jnp.max(scores[TOK:], axis=0, keepdims=True) + bias1,
    )
    weight = cat(
        [jnp.exp2(scores[:TOK] - (peak - bias0)), jnp.exp2(scores[TOK:] - (peak - bias1))], 0
    )
    prob = weight * (1.0 / jnp.sum(weight, axis=0, keepdims=True))
    term = prob * d_prob
    d_score = term - prob * jnp.sum(term, axis=0, keepdims=True)
    prob, d_score = split(prob), split(d_score)
    turned = [
        cat([cat([half[:, : 2 * TOK].T, half[:, 2 * TOK :].T], 1) for half in value], 0)
        for value in (prob, d_score)
    ]
    return cat(d_score, 0), turned[0], turned[1]


def gather(sides, soft):
    by_key, prob, by_query = soft
    out = []
    for side, right in ((sides[1], by_key), (sides[0], by_query), (sides[2], prob)):
        left = cat([side[0][:HEAD], side[1][:HEAD], side[0][HEAD:], side[1][HEAD:]], 0)
        both = mm(cat([left, left], 1), right)
        first, second = both[: 2 * HEAD, : 2 * TOK], both[2 * HEAD :, 2 * TOK :]
        out.append(cat([first[:HEAD] + first[HEAD:], second[:HEAD] + second[HEAD:]], 0))
    return out


def pair_sides(parts, pair):
    rows = slice(2 * HEAD * pair, 2 * HEAD * pair + 2 * HEAD)
    return [(part[0][rows], part[1][rows]) for part in parts[:3]]


def finish(grads, w_back):
    whole = cat([cat([g[p][n] for n in range(3) for p in range(2)], 0) for g in grads], 1)
    out = mm(w_back[...], cat(split(whole), 0))
    return [out[:, 2 * TOK * n : 2 * TOK * n + 2 * TOK].T for n in range(len(grads))]


def weight_forms(w_qkv, w_out, w_across, w_along, w_back):
    zeros = jnp.zeros((CH, CH), BF16)
    for n in range(2):
        rows = slice(CH * n, CH * n + CH)
        w_across[rows, :CH] = w_qkv[:, rows].T
        w_across[rows, CH:] = zeros
    w_across[2 * CH :, :CH] = zeros
    w_across[2 * CH :, CH:] = w_out[...]
    for n, scale in enumerate((LOG2E * SCALE, SCALE)):
        cols = slice(CH * n, CH * n + CH)
        halves = split(w_qkv[:, CH + CH * n : 2 * CH + CH * n].astype(F32) * scale)
        for half in range(2):
            w_along[CH * half : CH * half + CH, cols] = halves[half]
    for half in range(2):
        w_back[:, 3 * CH * half : 3 * CH * half + 3 * CH] = w_qkv[...]


WEIGHTS = [
    pltpu.VMEM((3 * CH, 2 * CH), BF16),
    pltpu.VMEM((2 * CH, 2 * CH), BF16),
    pltpu.VMEM((CH, 6 * CH), BF16),
]


STASH = [
    pltpu.VMEM((2, 10, CH, 2 * TOK), BF16),
    pltpu.VMEM((2, 2 * TOK, 4 * TOK), F32),
    pltpu.VMEM((3, 4 * TOK, 4 * TOK), BF16),
    pltpu.VMEM((6, 2 * HEAD, 2 * TOK), BF16),
    pltpu.VMEM((3, 3, 2 * HEAD, 2 * TOK), F32),
]


def run_windows(total, picks, feat, grad, result, weights, stash, before, after):
    ahead, scored, softened, sided, kept = stash
    groups = (total + GROUP - 1) // GROUP

    def place(n):
        pick = picks[jnp.clip(n, 0, total - 1)]
        return pick // 512, (pick // 2) % 256, pick % 2

    def window(ref, n):
        row, col, _ = place(n)
        value = ref[:, pl.ds(row, WIN), pl.ds(col, WIN), :]
        return value.reshape(2 * TOK, CH).astype(BF16)

    def projected(n):
        return project(
            [window(feat, n), window(feat, n + 1)], [window(grad, n), window(grad, n + 1)], weights
        )

    def put(n, value):
        row, col, _ = place(n)
        result[:, pl.ds(row, WIN), pl.ds(col, WIN), :] = value.reshape(2, WIN, WIN, CH)

    def stash_ahead(parts):
        for w in range(2):
            for n in range(5):
                for half in range(2):
                    ahead[w, 2 * n + half] = parts[w][n][half]
        scored[0], scored[1] = products(parts[0], 0)

    def close(first):
        soft = [softened[n] for n in range(3)]
        last = gather([(sided[2 * n], sided[2 * n + 1]) for n in range(3)], soft)
        held = [[kept[u, n] for n in range(3)] for u in range(3)]
        for n, value in enumerate(finish([held[:2], [held[2], last]], weights[2])):
            put(first - 2 + n, value)

    @pl.when(total > 0)
    def _():
        before(1)
        stash_ahead(projected(0))

    @pl.loop(0, groups)
    def _(i):
        first = i * GROUP
        before(first + GROUP + 1)
        parts = [
            [(ahead[w, 2 * n], ahead[w, 2 * n + 1]) for n in range(5)] for w in range(2)
        ] + [None, None]
        flags = [place(first + n)[2] for n in range(GROUP)]
        ready = {0: (scored[0], scored[1])}
        soft, done = {}, {}
        for u in range(2 * GROUP):
            if u < 2 * GROUP - 1:
                ready[u + 1] = products(parts[(u + 1) // 2], (u + 1) % 2)
            else:
                stash_ahead(following)
            soft[u] = soften(flags[u // 2], *ready.pop(u))
            if u == 0:
                close(first)
                parts[2:] = projected(first + 2)
            else:
                v = u - 1
                done[v] = gather(pair_sides(parts[v // 2], v % 2), soft.pop(v))
            if u == 4:
                outs = finish([[done[0], done[1]], [done[2], done[3]]], weights[2])
                for n, value in enumerate(outs):
                    put(first + n, value)
            if u == 5:
                following = projected(first + GROUP)
        end = soft.pop(2 * GROUP - 1)
        for n in range(3):
            softened[n] = end[n]
        for n, side in enumerate(pair_sides(parts[-1], 1)):
            sided[2 * n], sided[2 * n + 1] = side
        for n, u in enumerate((4, 5, 6)):
            for m in range(3):
                kept[n, m] = done[u][m]
        after(first + 2)

    @pl.when(total > 0)
    def _():
        close(groups * GROUP)


def side_columns(payload):
    view = payload[:, : payload.shape[1] - 1].astype(F32)
    return view.reshape(2, 2 * view.shape[1], WIN, CH)


def inner_kernel(
    code, left, right, feat_hbm, grad_hbm, w_qkv, w_out, out_hbm,
    feat_in, grad_in, feat, grad, result, picks, upto, marks, far_vector, own, far, in_sem, out_sem, code_sem,
    *held,
):
    weights, stash = held[:3], held[3:]
    rows, cols = feat_in.shape[1], feat_in.shape[2]
    chunks = rows // WIN
    wide = cols // WIN + 1

    def load(c, hbm, buf, which):
        part = pl.ds(c * WIN, WIN)
        return pltpu.make_async_copy(hbm.at[:, part], buf.at[:, part], in_sem.at[c, which])

    def store(s):
        part = pl.ds(s * WIN + HALF, WIN)
        return pltpu.make_async_copy(
            result.at[:, part, pl.ds(WIN, cols)], out_hbm.at[:, part], out_sem.at[s]
        )

    @pl.loop(0, chunks)
    def _(c):
        load(c, feat_hbm, feat_in, 0).start()
        load(c, grad_hbm, grad_in, 1).start()

    far_vector[...] = left[0, 0, rows // 4].astype(F32).astype(jnp.int32)
    code_copies = [
        pltpu.make_async_copy(code, own, code_sem.at[0]),
        pltpu.make_async_copy(far_vector, far, code_sem.at[1]),
    ]
    for copy in code_copies:
        copy.start()
    weight_forms(w_qkv, w_out, *weights)
    for n, frame in enumerate((feat, grad)):
        for side, at in ((left, HALF), (right, cols + WIN)):
            value = side_columns(side[n])
            for half in range(2):
                part = slice(half * (rows // 2), (half + 1) * (rows // 2))
                frame[:, part, at : at + HALF] = value[:, :, HALF * half : HALF * half + HALF]
    for copy in code_copies:
        copy.wait()

    def scan(a, count):
        for b in range(wide):
            value = far[a, wide - 2] if b == 0 else own[a, b - 1]
            picks[count] = ((a * WIN + HALF) * 256 + b * WIN + HALF) * 2 + value
            count = count + (value >= 0).astype(jnp.int32)
        upto[a] = count
        return count

    total = lax.fori_loop(0, chunks - 1, scan, jnp.int32(0))

    @pl.loop(0, chunks)
    def _(c):
        result[:, pl.ds(c * WIN, WIN)] = jnp.zeros((2, WIN) + result.shape[2:], F32)

    marks[0] = 0
    marks[1] = 0

    def convert(until):
        @pl.loop(marks[0], until)
        def _(c):
            load(c, feat_hbm, feat_in, 0).wait()
            load(c, grad_hbm, grad_in, 1).wait()
            part = pl.ds(c * WIN, WIN)
            feat[:, part, WIN : WIN + cols] = feat_in[:, part].astype(F32)
            grad[:, part, WIN : WIN + cols] = grad_in[:, part].astype(F32)

        marks[0] = jnp.maximum(marks[0], until)

    def before(n):
        row = picks[jnp.minimum(n, total - 1)] // 512
        convert((row + WIN - 1) // WIN + 1)

    def after(count):
        s = marks[1]
        full = (s < chunks - 1) & (upto[jnp.minimum(s, chunks - 2)] <= jnp.minimum(count, total - 1))

        @pl.when(full)
        def _():
            store(s).start()
            marks[1] = s + 1

    run_windows(total, picks, feat, grad, result, weights, stash, before, after)
    convert(chunks)

    @pl.loop(marks[1], chunks - 1)
    def _(s):
        store(s).start()

    @pl.loop(0, chunks - 1)
    def _(s):
        store(s).wait()


def inner_windows(code, left, right, features, grad_out, w_qkv, w_out):
    shape = features.shape
    chunks, wide = shape[1] // WIN, shape[2] // WIN + 1
    frame = (2, shape[1], shape[2] + 2 * WIN, CH)
    hbm = pl.BlockSpec(memory_space=pl.ANY)
    vmem = pl.BlockSpec(memory_space=pltpu.VMEM)
    return pl.pallas_call(
        inner_kernel,
        out_shape=jax.ShapeDtypeStruct(shape, F32),
        in_specs=[hbm, vmem, vmem, hbm, hbm, vmem, vmem],
        out_specs=hbm,
        scratch_shapes=[
            pltpu.VMEM(shape, BF16),
            pltpu.VMEM(shape, BF16),
            pltpu.VMEM(frame, F32),
            pltpu.VMEM(frame, F32),
            pltpu.VMEM(frame, F32),
            pltpu.SMEM((chunks * wide,), jnp.int32),
            pltpu.SMEM((chunks,), jnp.int32),
            pltpu.SMEM((2,), jnp.int32),
            pltpu.VMEM((2 * WIN, CH), jnp.int32),
            pltpu.SMEM(code.shape, jnp.int32),
            pltpu.SMEM((2 * WIN, CH), jnp.int32),
            pltpu.SemaphoreType.DMA((chunks, 2)),
            pltpu.SemaphoreType.DMA((chunks - 1,)),
            pltpu.SemaphoreType.DMA((2,)),
            *WEIGHTS,
            *STASH,
        ],
        compiler_params=pltpu.CompilerParams(vmem_limit_bytes=52 * 2**20),
        cost_estimate=pl.CostEstimate(flops=119 * 235 * 10**6, bytes_accessed=16 * 2**20, transcendentals=119 * 65536),
        name="inner_windows",
    )(code, left, right, features, grad_out, w_qkv, w_out)


def edge_kernel(
    code, above, below, left, right, feat_hbm, grad_hbm, w_qkv, w_out, before, out_hbm,
    rows_in, feat, grad, result, picks, far_vector, own, far, in_sem, code_sem, out_sem,
    *held,
):
    weights, stash = held[:3], held[3:]
    rows, cols = feat_hbm.shape[1], feat_hbm.shape[2]
    wide = cols // WIN + 1
    last_row, last_col = rows // WIN - 1, cols // WIN - 1
    copies = [
        pltpu.make_async_copy(hbm.at[:, pl.ds(at, HALF)], rows_in.at[n, m], in_sem.at[n, m])
        for n, hbm in enumerate((feat_hbm, grad_hbm))
        for m, at in enumerate((0, rows - HALF))
    ]
    for copy in copies:
        copy.start()
    far_vector[: 2 * WIN] = above[0, 0, 0, cols + 2 * WIN :].astype(F32).astype(jnp.int32)
    far_vector[2 * WIN :] = left[0, 0, rows // 4].astype(F32).astype(jnp.int32)
    code_copies = [
        pltpu.make_async_copy(code, own, code_sem.at[0]),
        pltpu.make_async_copy(far_vector, far, code_sem.at[1]),
    ]
    for copy in code_copies:
        copy.start()
    weight_forms(w_qkv, w_out, *weights)
    result[...] = jnp.zeros_like(result)
    for n, frame in enumerate((feat, grad)):
        frame[:, :HALF] = above[n, :, :, : cols + 2 * WIN].astype(F32)
        frame[:, 3 * HALF :] = below[n, :, :, : cols + 2 * WIN].astype(F32)
        for side, at in ((left, HALF), (right, cols + WIN)):
            for half, first in enumerate((0, rows // 4 - HALF // 2)):
                part = side[n, :, first : first + HALF // 2].astype(F32).reshape(2, HALF, WIN, CH)
                frame[:, HALF * (half + 1) : HALF * (half + 2), at : at + HALF] = part[
                    :, :, HALF * half : HALF * half + HALF
                ]
    for copy in code_copies:
        copy.wait()

    def pick(row, b, value, count):
        picks[count] = (row * 256 + b * WIN + HALF) * 2 + value
        return count + (value >= 0).astype(jnp.int32)

    total = pick(0, 0, far[WIN + last_row, last_col], jnp.int32(0))
    for b in range(1, wide):
        total = pick(0, b, far[last_row, b - 1], total)
    total = pick(WIN, 0, far[2 * WIN + last_row, last_col], total)
    for b in range(1, wide):
        total = pick(WIN, b, own[last_row, b - 1], total)

    for copy in copies:
        copy.wait()
    for n, frame in enumerate((feat, grad)):
        for m in range(2):
            frame[:, HALF * (m + 1) : HALF * (m + 2), WIN : WIN + cols] = rows_in[n, m].astype(F32)

    run_windows(
        total, picks, feat, grad, result, weights, stash,
        lambda n: None, lambda n: None,
    )
    back = [
        pltpu.make_async_copy(
            result.at[:, pl.ds(HALF * (m + 1), HALF), pl.ds(WIN, cols)],
            out_hbm.at[:, pl.ds(at, HALF)],
            out_sem.at[m],
        )
        for m, at in enumerate((0, rows - HALF))
    ]
    for copy in back:
        copy.start()
    for copy in back:
        copy.wait()


def edge_windows(code, halos, features, grad_out, w_qkv, w_out, before):
    shape = features.shape
    cols = shape[2]
    frame = (2, 2 * WIN, cols + 2 * WIN, CH)
    hbm = pl.BlockSpec(memory_space=pl.ANY)
    vmem = pl.BlockSpec(memory_space=pltpu.VMEM)
    operands = (code, *halos, features, grad_out, w_qkv, w_out, before)
    return pl.pallas_call(
        edge_kernel,
        out_shape=jax.ShapeDtypeStruct(shape, F32),
        in_specs=[hbm] + [vmem] * 4 + [hbm] * 2 + [vmem] * 2 + [hbm],
        out_specs=hbm,
        scratch_shapes=[
            pltpu.VMEM((2, 2, 2, HALF, cols, CH), BF16),
            pltpu.VMEM(frame, F32),
            pltpu.VMEM(frame, F32),
            pltpu.VMEM(frame, F32),
            pltpu.SMEM((2 * (cols // WIN + 1) + 1,), jnp.int32),
            pltpu.VMEM((4 * WIN, CH), jnp.int32),
            pltpu.SMEM(code.shape, jnp.int32),
            pltpu.SMEM((4 * WIN, CH), jnp.int32),
            pltpu.SemaphoreType.DMA((2, 2)),
            pltpu.SemaphoreType.DMA((2,)),
            pltpu.SemaphoreType.DMA((2,)),
            *WEIGHTS,
            *STASH,
        ],
        input_output_aliases={len(operands) - 1: 0},
        compiler_params=pltpu.CompilerParams(vmem_limit_bytes=52 * 2**20),
        cost_estimate=pl.CostEstimate(flops=34 * 235 * 10**6, bytes_accessed=4 * 2**20, transcendentals=34 * 65536),
        name="edge_windows",
    )(*operands)


def column_kernel(route, feat_hbm, grad_hbm, cross, west, east, code, cols_in, page, in_sem):
    rows, cols = feat_hbm.shape[1], feat_hbm.shape[2]
    copies = [
        pltpu.make_async_copy(
            hbm.at[:, :, pl.ds(at, 2 * WIN)], cols_in.at[n, m], in_sem.at[n, m]
        )
        for n, hbm in enumerate((feat_hbm, grad_hbm))
        for m, at in enumerate((0, cols - 2 * WIN))
    ]
    for copy in copies:
        copy.start()
    shape = cross.shape
    ids = lax.broadcasted_iota(jnp.int32, shape, 0) * shape[1] + lax.broadcasted_iota(jnp.int32, shape, 1)
    live = jnp.zeros(shape, jnp.int32)
    for d in range(route.shape[2]):
        for s in range(route.shape[3]):
            live = jnp.where(ids == route[0, 0, d, s], 1, live)
    value = jnp.where(live > 0, jnp.where(cross[...] > 0, 1, 0), -1)
    code[...] = jnp.full(code.shape, -1, jnp.int32)
    code[:, : shape[1]] = value
    page[...] = jnp.zeros_like(page)
    page[: shape[0], : shape[1]] = value.astype(F32)
    for out in (west, east):
        for n in range(2):
            for v in range(2):
                out[n, v, rows // 4] = page[...].astype(BF16)
    for copy in copies:
        copy.wait()
    upper = lax.broadcasted_iota(jnp.int32, (1, 1, WIN, CH), 2) < HALF
    for n in range(2):
        for m, out in enumerate((west, east)):
            edge = cols_in[n, m].astype(F32)[:, :, WIN * m : WIN * m + WIN]
            first, second = edge[:, : rows // 2], edge[:, rows // 2 :]
            if m == 0:
                value = jnp.where(upper, first, pltpu.roll(second, HALF, 2))
            else:
                value = jnp.where(upper, pltpu.roll(first, HALF, 2), second)
            out[n, :, : rows // 4] = value.reshape(2, rows // 4, 2 * WIN, CH).astype(BF16)


def pack_columns(features, grad_out, cross_live, route):
    _, rows, cols, _ = features.shape
    hbm = pl.BlockSpec(memory_space=pl.ANY)
    vmem = pl.BlockSpec(memory_space=pltpu.VMEM)
    smem = pl.BlockSpec(memory_space=pltpu.SMEM)
    edge = jax.ShapeDtypeStruct((2, 2, rows // 4 + 1, 2 * WIN, CH), BF16)
    return pl.pallas_call(
        column_kernel,
        out_shape=(edge, edge, jax.ShapeDtypeStruct((cross_live.shape[0], CH), jnp.int32)),
        in_specs=[smem, hbm, hbm, vmem],
        out_specs=(vmem, vmem, vmem),
        scratch_shapes=[
            pltpu.VMEM((2, 2, 2, rows, 2 * WIN, CH), BF16),
            pltpu.VMEM((2 * WIN, CH), F32),
            pltpu.SemaphoreType.DMA((2, 2)),
        ],
        compiler_params=pltpu.CompilerParams(vmem_limit_bytes=52 * 2**20),
        name="pack_columns",
    )(route, features, grad_out, cross_live)


def row_kernel(feat_hbm, grad_hbm, left, right, code, north, south, code_out, rows_in, page, in_sem):
    rows = feat_hbm.shape[1]
    copies = [
        pltpu.make_async_copy(hbm.at[:, pl.ds(at, HALF)], rows_in.at[n, m], in_sem.at[n, m])
        for n, hbm in enumerate((feat_hbm, grad_hbm))
        for m, at in enumerate((0, rows - HALF))
    ]
    for copy in copies:
        copy.start()
    code_out[...] = code[...]
    page[:WIN] = code[...].astype(F32)
    page[WIN:] = left[0, 0, rows // 4].astype(F32)[:WIN]
    for copy in copies:
        copy.wait()
    tail = jnp.broadcast_to(page[...], (2, HALF, 2 * WIN, CH))
    for n in range(2):
        for m, out in enumerate((north, south)):
            part = slice(0, HALF // 2) if m == 0 else slice(rows // 4 - HALF // 2, rows // 4)
            sides = [side[n, :, part].astype(F32).reshape(2, HALF, WIN, CH) for side in (left, right)]
            sides[m] = pltpu.roll(sides[m], HALF, 2)
            whole = cat([sides[0], rows_in[n, m].astype(F32), sides[1], tail], 2)
            out[n] = whole.astype(BF16)


def pack_rows(features, grad_out, left, right, code):
    _, rows, cols, _ = features.shape
    hbm = pl.BlockSpec(memory_space=pl.ANY)
    vmem = pl.BlockSpec(memory_space=pltpu.VMEM)
    edge = jax.ShapeDtypeStruct((2, 2, HALF, cols + 4 * WIN, CH), BF16)
    return pl.pallas_call(
        row_kernel,
        out_shape=(edge, edge, jax.ShapeDtypeStruct(code.shape, jnp.int32)),
        in_specs=[hbm, hbm, vmem, vmem, vmem],
        out_specs=(vmem, vmem, vmem),
        scratch_shapes=[
            pltpu.VMEM((2, 2, 2, HALF, cols, CH), BF16),
            pltpu.VMEM((2 * WIN, CH), F32),
            pltpu.SemaphoreType.DMA((2, 2)),
        ],
        compiler_params=pltpu.CompilerParams(vmem_limit_bytes=52 * 2**20),
        name="pack_rows",
    )(features, grad_out, left, right, code)


def moved(value, axis, steps):
    count = lax.axis_size(axis)
    return lax.ppermute(value, axis, [(n, (n + steps) % count) for n in range(count)])


def on_device(features, grad_out, w_qkv, w_out, cross_live, route):
    west, east, code = pack_columns(features, grad_out, cross_live, route.transpose(0, 1, 3, 2))
    left, right = moved(east, "col", 1), moved(west, "col", -1)
    north, south, code = pack_rows(features, grad_out, left, right, code)
    above, below = moved(south, "row", 1), moved(north, "row", -1)
    inner = inner_windows(code, left, right, features, grad_out, w_qkv, w_out)
    return edge_windows(code, (above, below, left, right), features, grad_out, w_qkv, w_out, inner)


def solution(mesh):
    return jax.shard_map(
        on_device,
        mesh=mesh,
        in_specs=(
            P(None, "row", "col", None),
            P(None, "row", "col", None),
            P(),
            P(),
            P("row", "col"),
            P("row", "col", None, None),
        ),
        out_specs=P(None, "row", "col", None),
        check_vma=False,
    )
```

```python
import functools
import math

import jax
import jax.numpy as jnp
from jax import lax
from jax.experimental import pallas as pl
from jax.experimental.pallas import tpu as pltpu
from jax.sharding import PartitionSpec as P

F32 = jnp.float32
BF16 = jnp.bfloat16
HEADS = 4
WIN = 8
HALF = 4
CH = 128
HEAD = CH // HEADS
TOK = WIN * WIN
GROUP = 16
TAIL = 4
NEG = -1e30
LOG2E = math.log2(math.e)
SCALE = 1.0 / math.sqrt(HEAD)


def split(value):
    high = value.astype(BF16)
    return high, (value - high.astype(F32)).astype(BF16)


def mm(a, b):
    return lax.dot_general(a, b, (((1,), (0,)), ((), ())), preferred_element_type=F32)


def mm_nt(a, b):
    return lax.dot_general(a, b, (((1,), (1,)), ((), ())), preferred_element_type=F32)


def cat(parts, axis):
    return jnp.concatenate(parts, axis=axis)


def head_pair_rows(high, low, pair):
    zero = jnp.zeros((HEAD, 2 * TOK), BF16)
    zeros = jnp.zeros((2 * HEAD, 4 * TOK), BF16)
    first, second = (slice(HEAD * h, HEAD * h + HEAD) for h in (2 * pair, 2 * pair + 1))
    top = [cat([high[first], zero], 1), cat([zero, high[second]], 1)]
    fix = [cat([low[first], zero], 1), cat([zero, low[second]], 1)]
    tail = fix + [zeros] if pair == 0 else [zeros] + fix
    return cat(top + top + tail, 0)


def pair_product(tokens, columns, pair):
    lanes = slice(2 * HEAD * pair, 2 * HEAD * pair + 2 * HEAD)
    left = cat([tokens[0][:, lanes], tokens[1][:, lanes], tokens[0]], 1)
    return mm(left, head_pair_rows(columns[0], columns[1], pair))


def across_parts(across):
    return [split(across[CH * n : CH * n + CH]) for n in range(3)]


def project(window_feats, window_grads, weights):
    w_across, w_along = weights[0][...], weights[1][...]
    feats = cat(window_feats, 0)
    across = mm(w_across, cat([cat([f.T for f in part], 1) for part in (window_feats, window_grads)], 0))
    along = mm(cat([feats, feats], 1), w_along)
    out = []
    for n in range(len(window_feats)):
        part = slice(2 * TOK * n, 2 * TOK * n + 2 * TOK)
        out.append(
            across_parts(across[:, part]) + [split(along[part, :CH]), split(along[part, CH:])]
        )
    return out


def products(parts, pair):
    query, _, cotangent, keys, values = parts
    return pair_product(keys, query, pair), pair_product(values, cotangent, pair)


def soften(flag, scores, d_prob):
    lane = lax.broadcasted_iota(jnp.int32, (1, 4 * TOK), 1) % (2 * TOK)
    drop = jnp.where(flag > 0, 0.0, NEG).astype(F32)
    bias0 = jnp.where(lane < TOK, 0.0, drop)
    bias1 = jnp.where(lane < TOK, drop, 0.0)
    peak = jnp.maximum(
        jnp.max(scores[:TOK], axis=0, keepdims=True) + bias0,
        jnp.max(scores[TOK:], axis=0, keepdims=True) + bias1,
    )
    weight = cat(
        [jnp.exp2(scores[:TOK] - (peak - bias0)), jnp.exp2(scores[TOK:] - (peak - bias1))], 0
    )
    prob = weight * (1.0 / jnp.sum(weight, axis=0, keepdims=True))
    term = prob * d_prob
    d_score = term - prob * jnp.sum(term, axis=0, keepdims=True)
    prob, d_score = split(prob), split(d_score)
    turned = [
        cat([cat([half[:, : 2 * TOK].T, half[:, 2 * TOK :].T], 1) for half in value], 0)
        for value in (prob, d_score)
    ]
    return cat(d_score, 0), turned[0], turned[1]


def gather(sides, soft):
    by_key, prob, by_query = soft
    out = []
    for side, right in ((sides[1], by_key), (sides[0], by_query), (sides[2], prob)):
        left = cat([side[0][:HEAD], side[1][:HEAD], side[0][HEAD:], side[1][HEAD:]], 0)
        both = mm(cat([left, left], 1), right)
        first, second = both[: 2 * HEAD, : 2 * TOK], both[2 * HEAD :, 2 * TOK :]
        out.append(cat([first[:HEAD] + first[HEAD:], second[:HEAD] + second[HEAD:]], 0))
    return out


def pair_sides(parts, pair):
    rows = slice(2 * HEAD * pair, 2 * HEAD * pair + 2 * HEAD)
    return [(part[0][rows], part[1][rows]) for part in parts[:3]]


def finish(grads, w_back):
    whole = cat([cat([g[p][n] for n in range(3) for p in range(2)], 0) for g in grads], 1)
    out = mm(w_back[...], cat(split(whole), 0))
    return [out[:, 2 * TOK * n : 2 * TOK * n + 2 * TOK].T for n in range(len(grads))]


def weight_forms(w_qkv, w_out, w_across, w_along, w_back):
    zeros = jnp.zeros((CH, CH), BF16)
    for n in range(2):
        rows = slice(CH * n, CH * n + CH)
        w_across[rows, :CH] = w_qkv[:, rows].T
        w_across[rows, CH:] = zeros
    w_across[2 * CH :, :CH] = zeros
    w_across[2 * CH :, CH:] = w_out[...]
    for n, scale in enumerate((LOG2E * SCALE, SCALE)):
        cols = slice(CH * n, CH * n + CH)
        halves = split(w_qkv[:, CH + CH * n : 2 * CH + CH * n].astype(F32) * scale)
        for half in range(2):
            w_along[CH * half : CH * half + CH, cols] = halves[half]
    for half in range(2):
        w_back[:, 3 * CH * half : 3 * CH * half + 3 * CH] = w_qkv[...]


WEIGHTS = [
    pltpu.VMEM((3 * CH, 2 * CH), BF16),
    pltpu.VMEM((2 * CH, 2 * CH), BF16),
    pltpu.VMEM((CH, 6 * CH), BF16),
]


STASH = [
    pltpu.VMEM((2, 10, CH, 2 * TOK), BF16),
    pltpu.VMEM((2, 2 * TOK, 4 * TOK), F32),
    pltpu.VMEM((3, 4 * TOK, 4 * TOK), BF16),
    pltpu.VMEM((6, 2 * HEAD, 2 * TOK), BF16),
    pltpu.VMEM((3, 3, 2 * HEAD, 2 * TOK), F32),
]


def run_windows(total, picks, feat, grad, result, weights, stash, before, after):
    ahead, scored, softened, sided, kept = stash
    whole = total // GROUP
    rest = (total % GROUP + TAIL - 1) // TAIL

    def place(n):
        pick = picks[jnp.clip(n, 0, total - 1)]
        return pick // 512, (pick // 2) % 256, pick % 2

    def window(ref, n):
        row, col, _ = place(n)
        value = ref[:, pl.ds(row, WIN), pl.ds(col, WIN), :]
        return value.reshape(2 * TOK, CH).astype(BF16)

    def projected(n):
        return project(
            [window(feat, n), window(feat, n + 1)], [window(grad, n), window(grad, n + 1)], weights
        )

    def put(n, value):
        row, col, _ = place(n)
        result[:, pl.ds(row, WIN), pl.ds(col, WIN), :] = value.reshape(2, WIN, WIN, CH)

    def stash_ahead(parts):
        for w in range(2):
            for n in range(5):
                for half in range(2):
                    ahead[w, 2 * n + half] = parts[w][n][half]
        scored[0], scored[1] = products(parts[0], 0)

    def close(first):
        soft = [softened[n] for n in range(3)]
        last = gather([(sided[2 * n], sided[2 * n + 1]) for n in range(3)], soft)
        held = [[kept[u, n] for n in range(3)] for u in range(3)]
        for n, value in enumerate(finish([held[:2], [held[2], last]], weights[2])):
            put(first - 2 + n, value)

    @pl.when(total > 0)
    def _():
        before(1)
        stash_ahead(projected(0))

    def step(first, size):
        before(first + size + 1)
        parts = [
            [(ahead[w, 2 * n], ahead[w, 2 * n + 1]) for n in range(5)] for w in range(2)
        ] + [None] * (size - 2)
        flags = [place(first + n)[2] for n in range(size)]
        ready = {0: (scored[0], scored[1])}
        soft, done = {}, {}
        for u in range(2 * size):
            if u < 2 * size - 1:
                ready[u + 1] = products(parts[(u + 1) // 2], (u + 1) % 2)
            else:
                stash_ahead(following)
            soft[u] = soften(flags[u // 2], *ready.pop(u))
            if u == 0:
                close(first)
            else:
                v = u - 1
                done[v] = gather(pair_sides(parts[v // 2], v % 2), soft.pop(v))
            if u % 4 == 0 and u < 2 * size - 4:
                parts[u // 2 + 2 : u // 2 + 4] = projected(first + u // 2 + 2)
            if u % 4 == 0 and u > 0:
                outs = finish([[done[u - 4], done[u - 3]], [done[u - 2], done[u - 1]]], weights[2])
                for n, value in enumerate(outs):
                    put(first + u // 2 - 2 + n, value)
            if u == 2 * size - 3:
                following = projected(first + size)
        end = soft.pop(2 * size - 1)
        for n in range(3):
            softened[n] = end[n]
        for n, side in enumerate(pair_sides(parts[-1], 1)):
            sided[2 * n], sided[2 * n + 1] = side
        for n, u in enumerate(range(2 * size - 4, 2 * size - 1)):
            for m in range(3):
                kept[n, m] = done[u][m]
        after(first + size - 2)

    @pl.loop(0, whole)
    def _(i):
        step(i * GROUP, GROUP)

    @pl.loop(0, rest)
    def _(i):
        step(whole * GROUP + i * TAIL, TAIL)

    @pl.when(total > 0)
    def _():
        close(whole * GROUP + rest * TAIL)


def side_columns(payload):
    view = payload[:, : payload.shape[1] - 1].astype(F32)
    return view.reshape(2, 2 * view.shape[1], WIN, CH)


def inner_kernel(
    code, left, right, feat_hbm, grad_hbm, w_qkv, w_out, out_hbm,
    feat_in, grad_in, feat, grad, result, picks, upto, marks, far_vector, own, far, in_sem, out_sem, code_sem,
    *held,
):
    weights, stash = held[:3], held[3:]
    rows, cols = feat_in.shape[1], feat_in.shape[2]
    chunks = rows // WIN
    wide = cols // WIN + 1

    def load(c, hbm, buf, which):
        part = pl.ds(c * WIN, WIN)
        return pltpu.make_async_copy(hbm.at[:, part], buf.at[:, part], in_sem.at[c, which])

    def store(s):
        part = pl.ds(s * WIN + HALF, WIN)
        return pltpu.make_async_copy(
            result.at[:, part, pl.ds(WIN, cols)], out_hbm.at[:, part], out_sem.at[s]
        )

    @pl.loop(0, chunks)
    def _(c):
        load(c, feat_hbm, feat_in, 0).start()
        load(c, grad_hbm, grad_in, 1).start()

    far_vector[...] = left[0, 0, rows // 4].astype(F32).astype(jnp.int32)
    code_copies = [
        pltpu.make_async_copy(code, own, code_sem.at[0]),
        pltpu.make_async_copy(far_vector, far, code_sem.at[1]),
    ]
    for copy in code_copies:
        copy.start()
    weight_forms(w_qkv, w_out, *weights)
    for n, frame in enumerate((feat, grad)):
        for side, at in ((left, HALF), (right, cols + WIN)):
            value = side_columns(side[n])
            for half in range(2):
                part = slice(half * (rows // 2), (half + 1) * (rows // 2))
                frame[:, part, at : at + HALF] = value[:, :, HALF * half : HALF * half + HALF]
    for copy in code_copies:
        copy.wait()

    end = picks.shape[0] - 1

    def scan(a, count):
        for b in range(wide):
            value = far[a, wide - 2] if b == 0 else own[a, b - 1]
            spot = (a * WIN + HALF) * 256 + b * WIN + HALF
            skipped = a * wide + b - count
            picks[count] = spot * 2 + value
            picks[end - skipped] = spot
            count = count + (value >= 0).astype(jnp.int32)
        upto[a] = count
        return count

    total = lax.fori_loop(0, chunks - 1, scan, jnp.int32(0))

    @pl.loop(0, (chunks - 1) * wide - total)
    def _(n):
        spot = picks[end - n]
        window = (slice(None), pl.ds(spot // 256, WIN), pl.ds(spot % 256, WIN))
        result[window] = jnp.zeros((2, WIN, WIN, CH), F32)

    marks[0] = 0
    marks[1] = 0

    def convert(until):
        @pl.loop(marks[0], until)
        def _(c):
            load(c, feat_hbm, feat_in, 0).wait()
            load(c, grad_hbm, grad_in, 1).wait()
            part = pl.ds(c * WIN, WIN)
            feat[:, part, WIN : WIN + cols] = feat_in[:, part].astype(F32)
            grad[:, part, WIN : WIN + cols] = grad_in[:, part].astype(F32)

        marks[0] = jnp.maximum(marks[0], until)

    def before(n):
        row = picks[jnp.minimum(n, total - 1)] // 512
        convert((row + WIN - 1) // WIN + 1)

    def after(count):
        s = marks[1]
        full = (s < chunks - 1) & (upto[jnp.minimum(s, chunks - 2)] <= jnp.minimum(count, total - 1))

        @pl.when(full)
        def _():
            store(s).start()
            marks[1] = s + 1

    run_windows(total, picks, feat, grad, result, weights, stash, before, after)
    convert(chunks)

    @pl.loop(marks[1], chunks - 1)
    def _(s):
        store(s).start()

    @pl.loop(0, chunks - 1)
    def _(s):
        store(s).wait()


def inner_windows(code, left, right, features, grad_out, w_qkv, w_out):
    shape = features.shape
    chunks, wide = shape[1] // WIN, shape[2] // WIN + 1
    frame = (2, shape[1], shape[2] + 2 * WIN, CH)
    hbm = pl.BlockSpec(memory_space=pl.ANY)
    vmem = pl.BlockSpec(memory_space=pltpu.VMEM)
    return pl.pallas_call(
        inner_kernel,
        out_shape=jax.ShapeDtypeStruct(shape, F32),
        in_specs=[hbm, vmem, vmem, hbm, hbm, vmem, vmem],
        out_specs=hbm,
        scratch_shapes=[
            pltpu.VMEM(shape, BF16),
            pltpu.VMEM(shape, BF16),
            pltpu.VMEM(frame, F32),
            pltpu.VMEM(frame, F32),
            pltpu.VMEM(frame, F32),
            pltpu.SMEM((chunks * wide,), jnp.int32),
            pltpu.SMEM((chunks,), jnp.int32),
            pltpu.SMEM((2,), jnp.int32),
            pltpu.VMEM((2 * WIN, CH), jnp.int32),
            pltpu.SMEM(code.shape, jnp.int32),
            pltpu.SMEM((2 * WIN, CH), jnp.int32),
            pltpu.SemaphoreType.DMA((chunks, 2)),
            pltpu.SemaphoreType.DMA((chunks - 1,)),
            pltpu.SemaphoreType.DMA((2,)),
            *WEIGHTS,
            *STASH,
        ],
        compiler_params=pltpu.CompilerParams(vmem_limit_bytes=52 * 2**20),
        cost_estimate=pl.CostEstimate(flops=119 * 235 * 10**6, bytes_accessed=16 * 2**20, transcendentals=119 * 65536),
        name="inner_windows",
    )(code, left, right, features, grad_out, w_qkv, w_out)


def edge_kernel(
    code, above, below, left, right, feat_hbm, grad_hbm, w_qkv, w_out, before, out_hbm,
    rows_in, feat, grad, result, picks, far_vector, own, far, in_sem, code_sem, out_sem,
    *held,
):
    weights, stash = held[:3], held[3:]
    rows, cols = feat_hbm.shape[1], feat_hbm.shape[2]
    wide = cols // WIN + 1
    last_row, last_col = rows // WIN - 1, cols // WIN - 1
    copies = [
        pltpu.make_async_copy(hbm.at[:, pl.ds(at, HALF)], rows_in.at[n, m], in_sem.at[n, m])
        for n, hbm in enumerate((feat_hbm, grad_hbm))
        for m, at in enumerate((0, rows - HALF))
    ]
    for copy in copies:
        copy.start()
    far_vector[: 2 * WIN] = above[0, 0, 0, cols + 2 * WIN :].astype(F32).astype(jnp.int32)
    far_vector[2 * WIN :] = left[0, 0, rows // 4].astype(F32).astype(jnp.int32)
    code_copies = [
        pltpu.make_async_copy(code, own, code_sem.at[0]),
        pltpu.make_async_copy(far_vector, far, code_sem.at[1]),
    ]
    for copy in code_copies:
        copy.start()
    weight_forms(w_qkv, w_out, *weights)
    result[...] = jnp.zeros_like(result)
    for n, frame in enumerate((feat, grad)):
        frame[:, :HALF] = above[n, :, :, : cols + 2 * WIN].astype(F32)
        frame[:, 3 * HALF :] = below[n, :, :, : cols + 2 * WIN].astype(F32)
        for side, at in ((left, HALF), (right, cols + WIN)):
            for half, first in enumerate((0, rows // 4 - HALF // 2)):
                part = side[n, :, first : first + HALF // 2].astype(F32).reshape(2, HALF, WIN, CH)
                frame[:, HALF * (half + 1) : HALF * (half + 2), at : at + HALF] = part[
                    :, :, HALF * half : HALF * half + HALF
                ]
    for copy in code_copies:
        copy.wait()

    def pick(row, b, value, count):
        picks[count] = (row * 256 + b * WIN + HALF) * 2 + value
        return count + (value >= 0).astype(jnp.int32)

    total = pick(0, 0, far[WIN + last_row, last_col], jnp.int32(0))
    for b in range(1, wide):
        total = pick(0, b, far[last_row, b - 1], total)
    total = pick(WIN, 0, far[2 * WIN + last_row, last_col], total)
    for b in range(1, wide):
        total = pick(WIN, b, own[last_row, b - 1], total)

    for copy in copies:
        copy.wait()
    for n, frame in enumerate((feat, grad)):
        for m in range(2):
            frame[:, HALF * (m + 1) : HALF * (m + 2), WIN : WIN + cols] = rows_in[n, m].astype(F32)

    run_windows(
        total, picks, feat, grad, result, weights, stash,
        lambda n: None, lambda n: None,
    )
    back = [
        pltpu.make_async_copy(
            result.at[:, pl.ds(HALF * (m + 1), HALF), pl.ds(WIN, cols)],
            out_hbm.at[:, pl.ds(at, HALF)],
            out_sem.at[m],
        )
        for m, at in enumerate((0, rows - HALF))
    ]
    for copy in back:
        copy.start()
    for copy in back:
        copy.wait()


def edge_windows(code, halos, features, grad_out, w_qkv, w_out, before):
    shape = features.shape
    cols = shape[2]
    frame = (2, 2 * WIN, cols + 2 * WIN, CH)
    hbm = pl.BlockSpec(memory_space=pl.ANY)
    vmem = pl.BlockSpec(memory_space=pltpu.VMEM)
    operands = (code, *halos, features, grad_out, w_qkv, w_out, before)
    return pl.pallas_call(
        edge_kernel,
        out_shape=jax.ShapeDtypeStruct(shape, F32),
        in_specs=[hbm] + [vmem] * 4 + [hbm] * 2 + [vmem] * 2 + [hbm],
        out_specs=hbm,
        scratch_shapes=[
            pltpu.VMEM((2, 2, 2, HALF, cols, CH), BF16),
            pltpu.VMEM(frame, F32),
            pltpu.VMEM(frame, F32),
            pltpu.VMEM(frame, F32),
            pltpu.SMEM((2 * (cols // WIN + 1) + 1,), jnp.int32),
            pltpu.VMEM((4 * WIN, CH), jnp.int32),
            pltpu.SMEM(code.shape, jnp.int32),
            pltpu.SMEM((4 * WIN, CH), jnp.int32),
            pltpu.SemaphoreType.DMA((2, 2)),
            pltpu.SemaphoreType.DMA((2,)),
            pltpu.SemaphoreType.DMA((2,)),
            *WEIGHTS,
            *STASH,
        ],
        input_output_aliases={len(operands) - 1: 0},
        compiler_params=pltpu.CompilerParams(vmem_limit_bytes=52 * 2**20),
        cost_estimate=pl.CostEstimate(flops=34 * 235 * 10**6, bytes_accessed=4 * 2**20, transcendentals=34 * 65536),
        name="edge_windows",
    )(*operands)


def column_kernel(route_hbm, feat_hbm, grad_hbm, cross_hbm, west, east, code, cols_in, page, route, cross, in_sem, small_sem):
    rows, cols = feat_hbm.shape[1], feat_hbm.shape[2]
    copies = [
        pltpu.make_async_copy(
            hbm.at[:, :, pl.ds(at, 2 * WIN)], cols_in.at[n, m], in_sem.at[n, m]
        )
        for n, hbm in enumerate((feat_hbm, grad_hbm))
        for m, at in enumerate((0, cols - 2 * WIN))
    ]
    small = [
        pltpu.make_async_copy(route_hbm, route, small_sem.at[0]),
        pltpu.make_async_copy(cross_hbm, cross, small_sem.at[1]),
    ]
    for copy in small + copies:
        copy.start()
    for copy in small:
        copy.wait()
    shape = cross.shape
    ids = lax.broadcasted_iota(jnp.int32, shape, 0) * shape[1] + lax.broadcasted_iota(jnp.int32, shape, 1)
    live = jnp.zeros(shape, jnp.int32)
    for d in range(route.shape[2]):
        for s in range(route.shape[3]):
            live = jnp.where(ids == route[0, 0, d, s], 1, live)
    value = jnp.where(live > 0, jnp.where(cross[...] > 0, 1, 0), -1)
    code[...] = jnp.full(code.shape, -1, jnp.int32)
    code[:, : shape[1]] = value
    page[...] = jnp.zeros_like(page)
    page[: shape[0], : shape[1]] = value.astype(F32)
    for out in (west, east):
        for n in range(2):
            for v in range(2):
                out[n, v, rows // 4] = page[...].astype(BF16)
    for copy in copies:
        copy.wait()
    upper = lax.broadcasted_iota(jnp.int32, (1, 1, WIN, CH), 2) < HALF
    for n in range(2):
        for m, out in enumerate((west, east)):
            edge = cols_in[n, m].astype(F32)[:, :, WIN * m : WIN * m + WIN]
            first, second = edge[:, : rows // 2], edge[:, rows // 2 :]
            if m == 0:
                value = jnp.where(upper, first, pltpu.roll(second, HALF, 2))
            else:
                value = jnp.where(upper, pltpu.roll(first, HALF, 2), second)
            out[n, :, : rows // 4] = value.reshape(2, rows // 4, 2 * WIN, CH).astype(BF16)


def pack_columns(features, grad_out, cross_live, route):
    _, rows, cols, _ = features.shape
    hbm = pl.BlockSpec(memory_space=pl.ANY)
    vmem = pl.BlockSpec(memory_space=pltpu.VMEM)
    smem = pl.BlockSpec(memory_space=pltpu.SMEM)
    edge = jax.ShapeDtypeStruct((2, 2, rows // 4 + 1, 2 * WIN, CH), BF16)
    return pl.pallas_call(
        column_kernel,
        out_shape=(edge, edge, jax.ShapeDtypeStruct((cross_live.shape[0], CH), jnp.int32)),
        in_specs=[hbm, hbm, hbm, hbm],
        out_specs=(vmem, vmem, vmem),
        scratch_shapes=[
            pltpu.VMEM((2, 2, 2, rows, 2 * WIN, CH), BF16),
            pltpu.VMEM((2 * WIN, CH), F32),
            pltpu.SMEM(route.shape, jnp.int32),
            pltpu.VMEM(cross_live.shape, jnp.int32),
            pltpu.SemaphoreType.DMA((2, 2)),
            pltpu.SemaphoreType.DMA((2,)),
        ],
        compiler_params=pltpu.CompilerParams(vmem_limit_bytes=60 * 2**20),
        name="pack_columns",
    )(route, features, grad_out, cross_live)


def row_kernel(feat_hbm, grad_hbm, left, right, code, north, south, code_out, rows_in, page, in_sem):
    rows = feat_hbm.shape[1]
    copies = [
        pltpu.make_async_copy(hbm.at[:, pl.ds(at, HALF)], rows_in.at[n, m], in_sem.at[n, m])
        for n, hbm in enumerate((feat_hbm, grad_hbm))
        for m, at in enumerate((0, rows - HALF))
    ]
    for copy in copies:
        copy.start()
    code_out[...] = code[...]
    page[:WIN] = code[...].astype(F32)
    page[WIN:] = left[0, 0, rows // 4].astype(F32)[:WIN]
    for copy in copies:
        copy.wait()
    tail = jnp.broadcast_to(page[...], (2, HALF, 2 * WIN, CH))
    for n in range(2):
        for m, out in enumerate((north, south)):
            part = slice(0, HALF // 2) if m == 0 else slice(rows // 4 - HALF // 2, rows // 4)
            sides = [side[n, :, part].astype(F32).reshape(2, HALF, WIN, CH) for side in (left, right)]
            sides[m] = pltpu.roll(sides[m], HALF, 2)
            whole = cat([sides[0], rows_in[n, m].astype(F32), sides[1], tail], 2)
            out[n] = whole.astype(BF16)


def pack_rows(features, grad_out, left, right, code):
    _, rows, cols, _ = features.shape
    hbm = pl.BlockSpec(memory_space=pl.ANY)
    vmem = pl.BlockSpec(memory_space=pltpu.VMEM)
    edge = jax.ShapeDtypeStruct((2, 2, HALF, cols + 4 * WIN, CH), BF16)
    return pl.pallas_call(
        row_kernel,
        out_shape=(edge, edge, jax.ShapeDtypeStruct(code.shape, jnp.int32)),
        in_specs=[hbm, hbm, vmem, vmem, vmem],
        out_specs=(vmem, vmem, vmem),
        scratch_shapes=[
            pltpu.VMEM((2, 2, 2, HALF, cols, CH), BF16),
            pltpu.VMEM((2 * WIN, CH), F32),
            pltpu.SemaphoreType.DMA((2, 2)),
        ],
        compiler_params=pltpu.CompilerParams(vmem_limit_bytes=52 * 2**20),
        name="pack_rows",
    )(features, grad_out, left, right, code)


def moved(value, axis, steps):
    count = lax.axis_size(axis)
    return lax.ppermute(value, axis, [(n, (n + steps) % count) for n in range(count)])


def on_device(features, grad_out, w_qkv, w_out, cross_live, route):
    west, east, code = pack_columns(features, grad_out, cross_live, route.transpose(0, 1, 3, 2))
    left, right = moved(east, "col", 1), moved(west, "col", -1)
    north, south, code = pack_rows(features, grad_out, left, right, code)
    above, below = moved(south, "row", 1), moved(north, "row", -1)
    inner = inner_windows(code, left, right, features, grad_out, w_qkv, w_out)
    return edge_windows(code, (above, below, left, right), features, grad_out, w_qkv, w_out, inner)


def solution(mesh):
    return jax.shard_map(
        on_device,
        mesh=mesh,
        in_specs=(
            P(None, "row", "col", None),
            P(None, "row", "col", None),
            P(),
            P(),
            P("row", "col"),
            P("row", "col", None, None),
        ),
        out_specs=P(None, "row", "col", None),
        check_vma=False,
    )
```
